512 devices in a mesh: occ: 8 (over z_hi, core), ao: 64 (over y, x, z_lo).
Axes of the slice: x: 4, y: 8, z: 8 (z_hi: 4, z_lo: 2; z = z_hi * 2 + z_lo), core: 2. Of those that a mesh axis runs over, the one named last changes fastest.
Arguments:
- integrals: bfloat16 [98304, 4096], P(('occ', 'ao')), may hold values from -0.5 to 0.5
- tile_owner: int32 [98304, 1], P(('occ', 'ao')), may hold values from 0 to 63; in each aligned block of 192 rows (0 to 191, 192 to 383, ...) at most 4 rows name the same one
- tile_blocks: int32 [98304, 3], P(('occ', 'ao')), may hold values from 0 to 255
- nu_offset: int32 [98304, 1], P(('occ', 'ao')), may hold values from 0 to 3
- pair_list: int32 [32, 2], replicated, may hold values from 0 to 255
- occ_coef: bfloat16 [2048, 256], P('ao'), may hold values from -6 to 6
- vir_coef: bfloat16 [2048, 1792], P('ao'), may hold values from -0.125 to 0.125
Outputs:
- exchange_ints: float32 [32, 1792, 1792], P('occ', 'ao')
The draws below stay inside these ranges and needn't reach their ends.
Inputs may be any that keep to these rules, and one draw needn't show every extreme that they name: `tile_owner`: among the rows of one device no value appears more than 4 times.
All inputs are finite; a program needn't handle non-finite values.
Results may differ from the reference program's by a relative error of at most 0.0048.
Values may be sent and summed in bfloat16 or wider, within the bound.
A program may use at most 64 MiB of HBM per device.

```python
import math
import jax
import jax.numpy as jnp
import numpy as np
from jax import lax

NAO = 2048
NOCC = 256
NVIR = 1792
SHELL_FUNCTIONS = 8
CAP = 4
TILES_DEV = 192
NBLK = 256
TILES = 98304
PAIR_TOTAL = 32
N_AO = 64


def set_ends(result, stream_key, low, top_value):
    index_at = [jax.random.randint(jax.random.fold_in(stream_key, axis), (), 0, length) for axis, length in enumerate(result.shape)]
    widest = result.shape.index(max(result.shape))
    next_to = index_at[:widest] + [(index_at[widest] + 1) % result.shape[widest]] + index_at[widest + 1:]
    return result.at[tuple(index_at)].set(low).at[tuple(next_to)].set(top_value)


def levels(rng, extent, split, smallest, largest):
    factor_of, own = 1.0, jax.random.fold_in(rng, 6)
    for axis_at, parts in split:
        steps = jnp.exp(jax.random.uniform(jax.random.fold_in(own, axis_at), (parts,), jnp.float32, smallest / len(split), largest / len(split)))
        factor_of = factor_of * jnp.repeat(steps, extent[axis_at] // parts).reshape([-1 if axis == axis_at else 1 for axis in range(len(extent))])
    return factor_of


def shared_out(key, own, number, rows, count, top, limit, lean):
    sequence = jax.random.permutation(key, count)
    crowded, usual = load_shares(count, rows * top, limit, lean, True), load_shares(count, rows * top, limit, lean, False)
    places = jnp.arange(count)

    def named(tallies, offset_by):
        used = int((tallies > 0).sum())
        fixed = max(1, used // 4)
        moved = fixed + (places - fixed + offset_by * (used - fixed)) % max(1, count - fixed)
        return jnp.zeros((count,), jnp.int32).at[sequence[jnp.where(places < fixed, places, moved)]].set(jnp.asarray(tallies, jnp.int32))

    tallies = jnp.where(number % 4 == 0, named(crowded, number // 4), named(usual, number - number // 4 - 1))
    mixed = jax.random.permutation(jax.random.fold_in(own, 3), count)
    donor, sink = mixed[0:count // 2 * 2:2], mixed[1:count // 2 * 2:2]
    slack = jnp.minimum(tallies[donor] - 1, limit - tallies[sink]) // 2
    slack = jnp.where((donor == sequence[0]) | (sink == sequence[0]) | (tallies[sink] == 0), 0, jnp.maximum(slack, 0))
    moved = jax.random.randint(jax.random.fold_in(own, 4), (count // 2,), 0, 1 << 20) % (slack + 1)
    tallies = tallies.at[donor].add(-moved).at[sink].add(moved)
    labels = jnp.searchsorted(jnp.cumsum(tallies), jnp.arange(rows * top), side="right").astype(jnp.int32)
    grid = labels.reshape(top, rows).T
    grid = grid[jax.random.permutation(jax.random.fold_in(own, 1), rows)]
    offset_by = jax.random.randint(jax.random.fold_in(own, 2), (rows, 1), 0, top)
    return jnp.take_along_axis(grid, (jnp.arange(top)[None, :] + offset_by) % top, axis=1)


def load_shares(amount, total, reach, slope, full):
    weights = [(1 << 20) // math.isqrt(standing ** slope) + 1 for standing in range(1, amount + 1)]
    largest = reach if full else min(reach, max(-(-total // amount), total * weights[0] // sum(weights)))
    least = 1 if total - largest >= amount - 1 else 0
    holding, spare = [largest] + [least] * (amount - 1), total - largest - least * (amount - 1)
    while spare > 0:
        candidates = [i for i in range(1, amount) if holding[i] < largest] or [i for i in range(1, amount) if holding[i] < reach]
        mass, budget = sum([weights[i] for i in candidates]), spare
        for i in candidates:
            addition = min(reach - holding[i], max(1, budget * weights[i] // mass), spare)
            holding[i] = holding[i] + addition
            spare = spare - addition
    return np.array(holding)


def noise(rng, extent, width, reach, split=(), dtype=jnp.bfloat16):
    drawn = width * jax.random.normal(rng, extent, jnp.float32)
    if split:
        drawn = drawn * levels(rng, extent, split, -0.22, 0.18)
    return jnp.clip(drawn, -reach, reach).astype(dtype)


def setup_inputs(seed: int = 0) -> dict:
    keys = jax.random.split(jax.random.key(seed), 8)
    integrals = noise(keys[0], (TILES, SHELL_FUNCTIONS ** 4), 0.0625, 0.5, ((0, 512),))
    tile_owner_keys = jax.random.split(jax.random.fold_in(keys[1], 1), TILES // TILES_DEV)
    tile_owner_turns = jax.random.permutation(jax.random.fold_in(keys[1], 3), TILES // TILES_DEV)
    tile_owner = jax.vmap(lambda own, number: shared_out(jax.random.fold_in(keys[1], 2), own, number, TILES_DEV, N_AO, 1, CAP, 2))(tile_owner_keys, tile_owner_turns).reshape((TILES, 1))
    tile_blocks = set_ends(jax.random.randint(keys[2], (TILES, 3), 0, NBLK), jax.random.fold_in(keys[2], 1), 0, NBLK - 1).astype(jnp.int32)
    nu_offset = set_ends(jax.random.randint(keys[3], (TILES, 1), 0, NBLK // N_AO), jax.random.fold_in(keys[3], 1), 0, (NBLK // N_AO) - 1).astype(jnp.int32)
    pair_list = set_ends(jax.random.randint(keys[4], (PAIR_TOTAL, 2), 0, NOCC), jax.random.fold_in(keys[4], 1), 0, NOCC - 1).astype(jnp.int32)
    occ_coef = noise(keys[5], (NAO, NOCC), 1.0, 6.0, ((0, 64),))
    vir_coef = noise(keys[6], (NAO, NVIR), NAO ** -0.5, 0.125, ((0, 64),))
    return {"integrals": integrals, "tile_owner": tile_owner, "tile_blocks": tile_blocks, "nu_offset": nu_offset, "pair_list": pair_list, "occ_coef": occ_coef, "vir_coef": vir_coef}


def reference(integrals, tile_owner, tile_blocks, nu_offset, pair_list, occ_coef, vir_coef):
    left_cols = jnp.take(occ_coef, pair_list[:, 0], axis=1).astype(jnp.float32)
    right_cols = jnp.take(occ_coef, pair_list[:, 1], axis=1).astype(jnp.float32)
    per_owner = NBLK // N_AO
    total_tiles = integrals.shape[0]
    group_width = TILES_DEV * 16
    group_count = total_tiles // group_width
    block_index = ((tile_owner[:, 0] * per_owner + nu_offset[:, 0]) * NBLK + tile_blocks[:, 2]).astype(jnp.int32)

    def accumulate(carry, members):
        tiles, bra_shells, ket_shells, targets = members
        left_row_block = jax.vmap(lambda offset: lax.dynamic_slice_in_dim(left_cols, offset, SHELL_FUNCTIONS, 0))(bra_shells * SHELL_FUNCTIONS)
        right_row_block = jax.vmap(lambda offset: lax.dynamic_slice_in_dim(right_cols, offset, SHELL_FUNCTIONS, 0))(ket_shells * SHELL_FUNCTIONS)
        density_matrix = jnp.einsum('ndy,noy->nydo', left_row_block, right_row_block).reshape(group_width, PAIR_TOTAL, SHELL_FUNCTIONS * SHELL_FUNCTIONS)
        partial_sums = jnp.einsum('tpk,tkn->tpn', density_matrix, tiles.astype(jnp.float32), precision=lax.Precision.HIGHEST)
        rounded = lax.optimization_barrier(partial_sums.astype(jnp.bfloat16)).astype(jnp.float32)
        return carry.at[targets].add(rounded), None

    members = (integrals.reshape(group_count, group_width, SHELL_FUNCTIONS * SHELL_FUNCTIONS, SHELL_FUNCTIONS * SHELL_FUNCTIONS),
               tile_blocks[:, 0].reshape(group_count, group_width),
               tile_blocks[:, 1].reshape(group_count, group_width),
               block_index.reshape(group_count, group_width))
    start_blocks = jnp.zeros((NBLK * NBLK, PAIR_TOTAL, SHELL_FUNCTIONS * SHELL_FUNCTIONS), jnp.float32)
    blocks, unused = lax.scan(accumulate, start_blocks, members)
    fields = blocks.reshape(NBLK, NBLK, PAIR_TOTAL, SHELL_FUNCTIONS, SHELL_FUNCTIONS).transpose(2, 0, 3, 1, 4).reshape(PAIR_TOTAL, NAO, NAO)

    def transform(field):
        half_field = field.astype(jnp.bfloat16)
        virtual_rows = jnp.dot(vir_coef.T, half_field.T, preferred_element_type=jnp.float32).astype(jnp.bfloat16)
        return jnp.dot(virtual_rows, vir_coef, preferred_element_type=jnp.float32)

    return lax.map(transform, fields)
```

```python
import jax
import jax.numpy as jnp
from jax import lax
from jax.experimental import pallas as pl
from jax.experimental.pallas import tpu as pltpu
from jax.sharding import PartitionSpec as P

SHELL_FUNCTIONS = 8
CAP = 4
NBLK = 256
NY, NX, NZ = 8, 4, 2
N_AO = 64
MESH = pl.DeviceIdType.MESH


def remote(src, dst, send, recv, occ, ao):
    return pltpu.make_async_remote_copy(
        src_ref=src, dst_ref=dst, send_sem=send, recv_sem=recv,
        device_id=(occ, ao), device_id_type=MESH,
    )


def gather_kernel(sel_ref, vir_ref, sel_out, vir_out, loc, sel_s, sel_r, y_s, y_r, z_s, z_r, x_s, x_r, c_s, c_r):
    occ = lax.axis_index("occ")
    ao = lax.axis_index("ao")
    half = lax.rem(occ, 2)
    sibling = occ + 1 - 2 * half
    zl = lax.rem(ao, NZ)
    x = lax.rem(ao // NZ, NX)
    y = ao // (NZ * NX)

    def ao_of(yy, xx, zz):
        return (yy * NX + xx) * NZ + zz

    barrier = pltpu.get_barrier_semaphore()

    def greet(k, carry):
        pl.semaphore_signal(barrier, inc=1, device_id=(occ, lax.rem(ao + k, N_AO)), device_id_type=MESH)
        return carry

    lax.fori_loop(1, N_AO, greet, 0)
    pl.semaphore_signal(barrier, inc=1, device_id=(sibling, ao), device_id_type=MESH)
    pl.semaphore_wait(barrier, N_AO)

    own = [
        pltpu.make_async_copy(sel_ref, sel_out.at[ao], loc.at[0]),
        pltpu.make_async_copy(vir_ref.at[half], vir_out.at[y, x, zl, half], loc.at[1]),
    ]
    for copy in own:
        copy.start()

    def y_copy(k):
        yy = lax.rem(y + k, NY)
        return remote(vir_ref.at[half], vir_out.at[y, x, zl, half], y_s.at[k], y_r.at[k], occ, ao_of(yy, x, zl))

    def sel_copy(k):
        return remote(sel_ref, sel_out.at[ao], sel_s.at[k], sel_r.at[k], occ, lax.rem(ao + k, N_AO))

    def start_sel(k, carry):
        sel_copy(k).start()
        return carry

    lax.fori_loop(1, N_AO, start_sel, 0)
    for k in range(1, NY):
        y_copy(k).start()
    for copy in own:
        copy.wait()
    for k in range(1, NY):
        y_copy(k).wait()
    z_copy = remote(vir_out.at[:, x, zl, half], vir_out.at[:, x, zl, half], z_s, z_r, occ, ao_of(y, x, 1 - zl))
    z_copy.start()
    z_copy.wait()
    right, left = lax.rem(x + 1, NX), lax.rem(x + NX - 1, NX)
    far = lax.rem(x + 2, NX)

    def x_copy(n, block, lo, hi, to):
        ref = vir_out.at[lo:hi, block, :, half]
        return remote(ref, ref, x_s.at[n], x_r.at[n], occ, ao_of(y, to, zl))

    def c_copy(n, block):
        ref = vir_out.at[:, block, :, half]
        return remote(ref, ref, c_s.at[n], c_r.at[n], sibling, ao)

    to_right = x_copy(0, x, 0, NY, right)
    to_left = x_copy(1, x, 0, NY, left)
    to_right.start()
    to_left.start()
    c_copies = [c_copy(0, x), c_copy(1, left), c_copy(2, right), c_copy(3, far)]
    to_right.wait_recv()
    fwd_right = x_copy(2, left, 0, NY // 2, right)
    fwd_right.start()
    to_left.wait_recv()
    fwd_left = x_copy(3, right, NY // 2, NY, left)
    fwd_left.start()
    for copy in c_copies[:3]:
        copy.start()
    to_right.wait_send()
    to_left.wait_send()
    fwd_right.wait()
    fwd_left.wait()
    c_copies[3].start()
    for copy in c_copies:
        copy.wait()

    def end_sel(k, carry):
        sel_copy(k).wait()
        return carry

    lax.fori_loop(1, N_AO, end_sel, 0)


def gather(sel, vir):
    dma = pltpu.SemaphoreType.DMA
    return pl.pallas_call(
        gather_kernel,
        out_shape=(
            jax.ShapeDtypeStruct((N_AO, 16, 128), jnp.bfloat16),
            jax.ShapeDtypeStruct((NY, NX, NZ, 2, 16, vir.shape[-1]), jnp.bfloat16),
        ),
        in_specs=[pl.BlockSpec(memory_space=pl.ANY)] * 2,
        out_specs=[pl.BlockSpec(memory_space=pl.ANY)] * 2,
        scratch_shapes=[
            dma((2,)), dma((N_AO,)), dma((N_AO,)), dma((NY,)), dma((NY,)), dma, dma,
            dma((4,)), dma((4,)), dma((4,)), dma((4,)),
        ],
        compiler_params=pltpu.CompilerParams(collective_id=0, has_side_effects=True),
    )(sel, vir)


def shell_rows(shell_ids, columns, shell_total):
    pair_count = columns.shape[1]
    flat_cols = columns.reshape(shell_total, SHELL_FUNCTIONS * pair_count)
    shell_table = jnp.arange(shell_total, dtype=jnp.int32)[None, :]
    picker = (shell_ids[:, None] == shell_table).astype(jnp.bfloat16)
    chosen = jnp.dot(picker, flat_cols, preferred_element_type=jnp.float32)
    return chosen.reshape(shell_ids.shape[0], SHELL_FUNCTIONS, pair_count)


def shards(integrals, tile_owner, tile_blocks, nu_offset, pair_list, occ_coef, vir_coef):
    ao_count = lax.axis_size("ao")
    occ_count = lax.axis_size("occ")
    orbital_count = occ_coef.shape[1]
    pair_count = pair_list.shape[0]
    orbital_ids = jnp.arange(orbital_count, dtype=jnp.int32)[:, None]
    both = jnp.concatenate([pair_list[:, 0], pair_list[:, 1]])
    pick = (orbital_ids == both[None, :]).astype(jnp.bfloat16)
    sel = jnp.dot(occ_coef, pick, preferred_element_type=jnp.float32).astype(jnp.bfloat16)
    sel = jnp.concatenate([sel[:16], sel[16:]], axis=1)
    cols, vir = gather(sel, vir_coef.reshape(2, 16, vir_coef.shape[1]))
    vir_full = vir.reshape(-1, vir_coef.shape[1])
    cols = cols.reshape(ao_count, 16, 2, 2 * pair_count).transpose(0, 2, 1, 3).reshape(-1, 2 * pair_count)
    left_cols = cols[:, :pair_count]
    right_cols = cols[:, pair_count:]
    tile_count = integrals.shape[0]
    tile_mats = integrals.reshape(
        tile_count, SHELL_FUNCTIONS * SHELL_FUNCTIONS, SHELL_FUNCTIONS * SHELL_FUNCTIONS
    )
    left_row_block = shell_rows(tile_blocks[:, 0], left_cols, NBLK)
    right_row_block = shell_rows(tile_blocks[:, 1], right_cols, NBLK)
    density_matrix = jnp.einsum("ndy,noy->nydo", left_row_block, right_row_block).reshape(
        tile_count, pair_count, SHELL_FUNCTIONS * SHELL_FUNCTIONS
    )
    product = jnp.einsum(
        "tpk,tkn->tpn",
        density_matrix,
        tile_mats.astype(jnp.float32),
        precision=lax.Precision.HIGHEST,
    )
    partial_rows = product.astype(jnp.bfloat16)
    owners = tile_owner[:, 0]
    order_ids = jnp.arange(tile_count, dtype=jnp.int32)
    earlier_same = (owners[:, None] == owners[None, :]) & (order_ids[None, :] < order_ids[:, None])
    slot_index = jnp.sum(earlier_same.astype(jnp.int32), axis=1)
    per_owner = NBLK // ao_count
    pairs_local = pair_count // occ_count
    destination = owners * CAP + slot_index
    slot_table = jnp.arange(ao_count * CAP, dtype=jnp.int32)[:, None]
    dispatch = slot_table == destination[None, :]
    flat_rows = partial_rows.reshape(tile_count, pair_count * SHELL_FUNCTIONS * SHELL_FUNCTIONS)
    outgoing = jnp.dot(
        dispatch.astype(jnp.bfloat16), flat_rows, preferred_element_type=jnp.float32
    ).astype(jnp.bfloat16)
    outgoing = outgoing.reshape(
        ao_count, CAP, occ_count, pairs_local * SHELL_FUNCTIONS * SHELL_FUNCTIONS
    )
    block_ids = nu_offset[:, 0] * NBLK + tile_blocks[:, 2]
    slot_ids = jnp.sum(jnp.where(dispatch, block_ids[None, :], 0), axis=1)
    outgoing_ids = jnp.broadcast_to(
        slot_ids.reshape(ao_count, CAP, 1, 1), (ao_count, CAP, occ_count, 1)
    )
    received, received_ids = (
        lax.all_to_all(
            lax.all_to_all(outgoing, "ao", split_axis=0, concat_axis=1, tiled=True),
            "occ",
            split_axis=2,
            concat_axis=1,
            tiled=True,
        ),
        lax.all_to_all(
            lax.all_to_all(outgoing_ids, "ao", split_axis=0, concat_axis=1, tiled=True),
            "occ",
            split_axis=2,
            concat_axis=1,
            tiled=True,
        ),
    )
    received_ids = received_ids.reshape(-1)
    received = received.reshape(
        received_ids.shape[0], pairs_local * SHELL_FUNCTIONS * SHELL_FUNCTIONS
    )
    target_table = jnp.arange(per_owner * NBLK, dtype=jnp.int32)[:, None]
    collector = (target_table == received_ids[None, :]).astype(jnp.bfloat16)
    sums = jnp.dot(collector, received, preferred_element_type=jnp.float32)
    half_field = sums.reshape(
        per_owner, NBLK, pairs_local, SHELL_FUNCTIONS, SHELL_FUNCTIONS
    ).transpose(2, 0, 3, 1, 4)
    half_field = half_field.reshape(
        pairs_local, per_owner * SHELL_FUNCTIONS, NBLK * SHELL_FUNCTIONS
    ).astype(jnp.bfloat16)
    virtual_rows = jnp.einsum(
        "pns,sb->pbn", half_field, vir_full, preferred_element_type=jnp.float32
    ).astype(jnp.bfloat16)
    return jnp.einsum(
        "pbn,na->pba",
        lax.all_to_all(virtual_rows, "ao", split_axis=1, concat_axis=2, tiled=True),
        vir_full,
        preferred_element_type=jnp.float32,
    )


def solution(mesh):
    placed = (
        P(("occ", "ao"), None),
        P(("occ", "ao"), None),
        P(("occ", "ao"), None),
        P(("occ", "ao"), None),
        P(),
        P("ao", None),
        P("ao", None),
    )
    return jax.shard_map(
        shards, mesh=mesh, in_specs=placed, out_specs=P("occ", "ao", None), check_vma=False
    )
```

```python
import jax
import jax.numpy as jnp
from jax import lax
from jax.experimental import pallas as pl
from jax.experimental.pallas import tpu as pltpu
from jax.sharding import PartitionSpec as P

NY, NX, NZ = 8, 4, 2
N_AO, N_OCC = 64, 8
TILES = 192
LANES = 256
CAP = 4
SLOTS = N_OCC * CAP
PAIRS = 32
P_LOC = PAIRS // N_OCC
NVIR = 1792
B_LOC = NVIR // N_AO
B_PAD = 32
CHUNK = 256
MESH = pl.DeviceIdType.MESH
F32, BF16, I32 = jnp.float32, jnp.bfloat16, jnp.int32


def remote(src, dst, send, recv, occ, ao):
    return pltpu.make_async_remote_copy(
        src_ref=src, dst_ref=dst, send_sem=send, recv_sem=recv,
        device_id=(occ, ao), device_id_type=MESH,
    )


def dot(a, b, dims=((1,), (0,))):
    return lax.dot_general(a, b, (dims, ((), ())), preferred_element_type=F32)


def iota(shape, dim):
    return lax.broadcasted_iota(I32, shape, dim)


def each(lo, hi, body, unroll=1):
    def step(k, carry):
        body(k)
        return carry

    lax.fori_loop(lo, hi, step, 0, unroll=unroll)


def kernel(
    ints_ref, owner_ref, blocks_ref, nuo_ref, pairs_ref, occ_ref, vir_ref,
    out_ref,
    cols, cols_f, vir, virp, flat, diag, expand, dens, part, s1, r1, meta, ids_o, sf, s2, r2, ids_s, ids_r,
    hot, hf, hb, vt, vs, vd, lhs,
    g_s, g_r, y_s, y_r, z_s, z_r, x_s, x_r, c_s, c_r, m_s, m_r, a_s, a_r, b_s, b_r, i_s, i_r, v_s, v_r,
):
    occ = lax.axis_index("occ")
    ao = lax.axis_index("ao")
    half = lax.rem(occ, 2)
    sibling = occ + 1 - 2 * half
    zl = lax.rem(ao, NZ)
    x = lax.rem(ao // NZ, NX)
    y = ao // (NZ * NX)

    def ao_of(yy, xx, zz):
        return (yy * NX + xx) * NZ + zz

    def ao_to(k):
        return lax.rem(ao + k, N_AO)

    def occ_to(k):
        return lax.rem(occ + k, N_OCC)

    barrier = pltpu.get_barrier_semaphore()

    def greet_ao(k):
        pl.semaphore_signal(barrier, inc=1, device_id=(occ, ao_to(k)), device_id_type=MESH)

    def greet_occ(k):
        pl.semaphore_signal(barrier, inc=1, device_id=(occ_to(k), ao), device_id_type=MESH)

    each(1, N_OCC, greet_occ)
    each(1, N_AO, greet_ao)

    pick = (iota((256, 128), 0) == jnp.broadcast_to(pairs_ref[...], (256, 128))).astype(F32).astype(BF16)
    sel = dot(occ_ref[...], pick)
    cols[ao] = jnp.where(iota((16, 128), 1) < 64, sel[:16], sel[16:]).astype(BF16)

    def padded(row, fill):
        return jnp.concatenate([row.astype(F32), jnp.full((1, LANES - TILES), fill, F32)], axis=1)

    owner = padded(owner_ref[...], -1.0)
    mu = blocks_ref[0:1]
    la = blocks_ref[1:2]
    rows = jnp.concatenate(
        [
            owner,
            padded((mu // 4) * 2 + mu % 2, -1.0),
            padded((mu // 2) % 2, 0.0),
            padded((la // 4) * 2 + la % 2, -1.0),
            padded((la // 2) % 2, 0.0),
            jnp.zeros((3, LANES), F32),
        ],
        axis=0,
    )
    upright = jnp.concatenate([rows, jnp.zeros((120, LANES), F32)], axis=0).T
    same = (upright[:, 0:1] == owner) & (iota((LANES, LANES), 0) < iota((LANES, LANES), 1))
    rank = jnp.sum(jnp.where(same, 1.0, 0.0), axis=0, keepdims=True)
    key = jnp.where(owner < 0.0, 256.0, rank * N_AO + owner)
    meta[occ] = jnp.concatenate(
        [key, padded(blocks_ref[2:3], 0.0), padded(nuo_ref[...], 0.0), jnp.zeros((5, LANES), F32)], axis=0
    )

    pl.semaphore_wait(barrier, N_AO + N_OCC - 2)

    def g_copy(k):
        return remote(cols.at[ao], cols.at[ao], g_s.at[k], g_r.at[k], occ, ao_to(k))

    def m_copy(k):
        return remote(meta.at[occ], meta.at[occ], m_s.at[k], m_r.at[k], occ_to(k), ao)

    def y_copy(k):
        return remote(
            vir_ref.at[half], vir.at[y, x, zl, half], y_s.at[k], y_r.at[k], occ, ao_of(lax.rem(y + k, NY), x, zl)
        )

    each(1, N_AO, lambda k: g_copy(k).start())
    each(1, N_OCC, lambda k: m_copy(k).start())
    each(1, NY, lambda k: y_copy(k).start())
    vir[y, x, zl, half] = vir_ref[half]

    def expansion(n):
        k = iota((1024, 128), 1) % 64
        p = n * 2 + iota((1024, 128), 1) // 64
        d = iota((1024, 128), 0) // 128
        hit = (iota((1024, 128), 0) % 32) == p
        left = hit & (d == (k % 32) // 4)
        right = hit & (d == (k % 4) * 2 + k // 32)
        expand[0, n] = jnp.where(left, 1.0, 0.0).astype(BF16)
        expand[1, n] = jnp.where(right, 1.0, 0.0).astype(BF16)

    each(0, 16, expansion)

    for kk in range(32):
        flat[kk * TILES:(kk + 1) * TILES] = ints_ref[:, kk * 128:(kk + 1) * 128].astype(F32)
    low = iota((32, 128), 1) < 64

    def place(t):
        block = flat[pl.ds(t, 32, stride=TILES), :]
        turned = pltpu.roll(block, 64, 1)
        zero = jnp.zeros_like(block)
        diag[t] = jnp.concatenate(
            [
                jnp.where(low, block, zero),
                jnp.where(low, turned, zero),
                jnp.where(low, zero, turned),
                jnp.where(low, zero, block),
            ],
            axis=0,
        ).astype(BF16)

    each(0, TILES, place, unroll=4)

    each(1, NY, lambda k: y_copy(k).wait())
    z_ref = vir.at[:, x, zl, half]
    z_copy = remote(z_ref, z_ref, z_s, z_r, occ, ao_of(y, x, 1 - zl))
    z_copy.start()

    each(1, N_AO, lambda k: g_copy(k).wait())
    cols_f[...] = cols[...].astype(F32).reshape(N_AO * 16, 128)
    table = jnp.concatenate(
        [cols_f[pl.ds(d, 128, stride=8), :].astype(BF16) for d in range(8)], axis=1
    )

    lane = iota((TILES, 1024), 1)

    def chosen(which):
        at = upright[:TILES, 1 + 2 * which:2 + 2 * which]
        part_of = upright[:TILES, 2 + 2 * which:3 + 2 * which]
        hot_rows = (iota((TILES, 128), 1).astype(F32) == at)
        got = dot(jnp.where(hot_rows, 1.0, 0.0).astype(BF16), table)
        keep = ((lane // 64) % 2).astype(F32) == part_of
        keep = keep & ((lane // 32) % 2 == which)
        return jnp.where(keep, got, 0.0).astype(BF16)

    left = chosen(0)
    right = chosen(1)
    for n in range(16):
        dens[n * TILES:(n + 1) * TILES] = dot(left, expand[0, n]) * dot(right, expand[1, n])

    def multiply(t):
        d = dens[pl.ds(t, 16, stride=TILES), :]
        hi = d.astype(BF16)
        lo = (d - hi.astype(F32)).astype(BF16)
        got = dot(jnp.concatenate([hi, lo], axis=0), diag[t])
        part[pl.ds(t, 16, stride=TILES), :] = got[:16] + got[16:]

    each(0, TILES, multiply, unroll=8)
    for n in range(16):
        s1[n // 2, :, (n % 2) * 128:(n % 2 + 1) * 128] = part[n * TILES:(n + 1) * TILES].astype(BF16)

    def a_copy(k):
        return remote(s1.at[occ_to(k)], r1.at[occ], a_s.at[k], a_r.at[k], occ_to(k), ao)

    each(1, N_OCC, lambda k: a_copy(k).start())
    r1[occ] = s1[occ]

    z_copy.wait()
    to_r, to_l, far = lax.rem(x + 1, NX), lax.rem(x + NX - 1, NX), lax.rem(x + 2, NX)

    def x_copy(n, block, lo, hi, to):
        ref = vir.at[lo:hi, block, :, half]
        return remote(ref, ref, x_s.at[n], x_r.at[n], occ, ao_of(y, to, zl))

    def c_copy(n, block):
        ref = vir.at[:, block, :, half]
        return remote(ref, ref, c_s.at[n], c_r.at[n], sibling, ao)

    x_copies = [
        x_copy(0, x, 0, NY, to_r),
        x_copy(1, x, 0, NY, to_l),
        x_copy(2, to_l, 0, NY // 2, to_r),
        x_copy(3, to_r, NY // 2, NY, to_l),
    ]
    c_copies = [c_copy(0, x), c_copy(1, to_l), c_copy(2, to_r), c_copy(3, far)]
    x_copies[0].start()
    x_copies[1].start()
    c_copies[0].start()

    each(1, N_OCC, lambda k: m_copy(k).wait())

    def sort(k):
        o = lax.rem(occ + N_OCC - k, N_OCC)

        @pl.when(k > 0)
        def _():
            a_copy(k).wait_recv()

        info = meta[o]
        hot_slots = jnp.where(
            iota((256, LANES), 0).astype(F32) == info[0:1], 1.0, 0.0
        ).astype(BF16)
        got = dot(hot_slots[:, :TILES], r1[o])
        for r in range(CAP):
            for n in range(2):
                sf[n, pl.ds(r * N_OCC + o, N_AO, stride=SLOTS), :] = got[r * 64:(r + 1) * 64, n * 128:(n + 1) * 128]
        names = dot(info.astype(BF16), hot_slots, ((1,), (1,)))
        ids_o[pl.ds(o, 1), :] = names[2:3] * 256.0 + names[1:2]

    each(0, N_OCC, sort)
    for n in range(2):
        s2[:, :, n * 128:(n + 1) * 128] = sf[n].astype(BF16).reshape(N_AO, SLOTS, 128)
    turned_ids = jnp.concatenate([ids_o[...], jnp.zeros((120, 256), F32)], axis=0).T
    wide = jnp.zeros((N_AO, 128), F32)
    for r in range(CAP):
        wide = wide + pltpu.roll(turned_ids[r * 64:(r + 1) * 64], r * N_OCC, 1)
    ids_s[...] = wide.reshape(N_AO, 1, 128)

    def b_copy(k):
        return remote(s2.at[ao_to(k)], r2.at[ao], b_s.at[k], b_r.at[k], occ, ao_to(k))

    def i_copy(k):
        return remote(ids_s.at[ao_to(k)], ids_r.at[ao], i_s.at[k], i_r.at[k], occ, ao_to(k))

    def start_b(k):
        i_copy(k).start()
        b_copy(k).start()

    each(1, N_AO, start_b)
    r2[ao] = s2[ao]
    ids_r[ao] = ids_s[ao]

    x_copies[0].wait_recv()
    x_copies[2].start()
    x_copies[1].wait_recv()
    x_copies[3].start()
    c_copies[1].start()
    c_copies[2].start()
    x_copies[2].wait_recv()
    x_copies[3].wait_recv()
    c_copies[3].start()
    for n in range(4):
        c_copies[n].wait_recv()

    order = jnp.where(
        iota((256, 256), 1) == (iota((256, 256), 0) % 32) * 8 + iota((256, 256), 0) // 32, 1.0, 0.0
    ).astype(BF16)

    def chunk(n):
        return pl.ds(pl.multiple_of(n * CHUNK, CHUNK), CHUNK)

    def reorder(n):
        for j in range(NY):
            got = dot(order, vir[j, :, :, :, :, chunk(n)].reshape(256, CHUNK)).astype(BF16)
            for si in range(8):
                virp[si * 256 + j * 32:si * 256 + (j + 1) * 32, chunk(n)] = got[si * 32:(si + 1) * 32]

    each(0, NVIR // CHUNK, reorder)

    def end_b(k):
        i_copy(k).wait()
        b_copy(k).wait()

    each(1, N_AO, end_b)

    def mark(s):
        names = jnp.broadcast_to(ids_r[s], (SLOTS, 128))
        name = jnp.sum(jnp.where(iota((SLOTS, 128), 0) == iota((SLOTS, 128), 1), names, 0.0), axis=1, keepdims=True)
        hot[s] = jnp.where(iota((SLOTS, 1024), 1).astype(F32) == name, 1.0, 0.0).astype(BF16)

    each(0, N_AO, mark, unroll=2)
    got_rows = r2[...].reshape(N_AO * SLOTS, 256)
    for n in range(4):
        total = dot(got_rows, hot[:, :, n * 256:(n + 1) * 256].reshape(N_AO * SLOTS, 256), ((0,), (0,)))
        hf[2 * n] = total[:, :128]
        hf[2 * n + 1] = total[:, 128:]
    for si in range(8):
        for m in range(2):
            hb[:, si * 256 + m * 128:si * 256 + (m + 1) * 128] = jnp.concatenate(
                [hf[2 * n + m, pl.ds(p * 64 + si, 8, stride=8), :] for p in range(P_LOC) for n in range(4)], axis=0
            ).astype(BF16)

    def first(n):
        rows_v = dot(hb[...], virp[:, chunk(n)]).astype(BF16).astype(F32)
        vt[chunk(n)] = rows_v.T

    each(0, NVIR // CHUNK, first)
    vt[NVIR:] = jnp.zeros((8, 128), F32)
    for s in range(N_AO):
        vs[s] = vt[s * B_LOC:s * B_LOC + B_PAD].astype(BF16)

    def v_copy(k):
        return remote(vs.at[ao_to(k)], vd.at[ao], v_s.at[k], v_r.at[k], occ, ao_to(k))

    each(1, N_AO, lambda k: v_copy(k).start())
    vd[ao] = vs[ao]
    each(1, N_AO, lambda k: v_copy(k).wait())

    quarter = iota((B_PAD, 128), 1) // 32

    def regroup(g):
        got = [vd[4 * g + s].astype(F32) for s in range(4)]
        for p in range(P_LOC):
            mixed = jnp.zeros((B_PAD, 128), F32)
            for s in range(4):
                shift = ((s - p) % 4) * 32
                piece = pltpu.roll(got[s], shift, 1) if shift else got[s]
                mixed = jnp.where(quarter == s, piece, mixed)
            lhs[g // 2, p * B_PAD:(p + 1) * B_PAD, pl.ds(pl.multiple_of((g % 2) * 128, 128), 128)] = mixed.astype(BF16)

    each(0, N_AO // 4, regroup, unroll=2)

    def second(n):
        total = jnp.zeros((P_LOC * B_PAD, CHUNK), F32)
        for j in range(NY):
            total = total + dot(lhs[j], vir[j, :, :, :, :, chunk(n)].reshape(256, CHUNK))
        for p in range(P_LOC):
            out_ref[p, :, chunk(n)] = total[p * B_PAD:p * B_PAD + B_LOC]

    each(0, NVIR // CHUNK, second)

    each(1, N_OCC, lambda k: a_copy(k).wait_send())
    for n in range(4):
        x_copies[n].wait_send()
        c_copies[n].wait_send()


def shards(integrals, tile_owner, tile_blocks, nu_offset, pair_list, occ_coef, vir_coef):
    pairs = jnp.tile(pair_list.T.reshape(1, 2 * PAIRS), (1, 2))
    dma = pltpu.SemaphoreType.DMA
    vmem = pltpu.VMEM
    return pl.pallas_call(
        kernel,
        out_shape=jax.ShapeDtypeStruct((P_LOC, B_LOC, NVIR), F32),
        in_specs=[pl.BlockSpec(memory_space=pltpu.VMEM)] * 7,
        out_specs=pl.BlockSpec(memory_space=pltpu.VMEM),
        scratch_shapes=[
            vmem((N_AO, 16, 128), BF16),
            vmem((N_AO * 16, 128), F32),
            vmem((NY, NX, NZ, 2, 16, NVIR), BF16),
            vmem((N_AO * 32, NVIR), BF16),
            vmem((32 * TILES, 128), F32),
            vmem((TILES, 128, 128), BF16),
            vmem((2, 16, 1024, 128), BF16),
            vmem((16 * TILES, 128), F32),
            vmem((16 * TILES, 128), F32),
            vmem((N_OCC, TILES, 256), BF16),
            vmem((N_OCC, TILES, 256), BF16),
            vmem((N_OCC, 8, LANES), F32),
            vmem((N_OCC, 256), F32),
            vmem((2, N_AO * SLOTS, 128), F32),
            vmem((N_AO, SLOTS, 256), BF16),
            vmem((N_AO, SLOTS, 256), BF16),
            vmem((N_AO, 1, 128), F32),
            vmem((N_AO, 1, 128), F32),
            vmem((N_AO, SLOTS, 1024), BF16),
            vmem((8, 256, 128), F32),
            vmem((128, 2048), BF16),
            vmem((NVIR + 8, 128), F32),
            vmem((N_AO, B_PAD, 128), BF16),
            vmem((N_AO, B_PAD, 128), BF16),
            vmem((NY, 128, 256), BF16),
            dma((N_AO,)), dma((N_AO,)), dma((NY,)), dma((NY,)), dma, dma,
            dma((4,)), dma((4,)), dma((4,)), dma((4,)), dma((N_OCC,)), dma((N_OCC,)), dma((N_OCC,)), dma((N_OCC,)),
            dma((N_AO,)), dma((N_AO,)), dma((N_AO,)), dma((N_AO,)), dma((N_AO,)), dma((N_AO,)),
        ],
        compiler_params=pltpu.CompilerParams(
            collective_id=0, has_side_effects=True, vmem_limit_bytes=60 * 1024 * 1024
        ),
    )(
        integrals, tile_owner.T, tile_blocks.T, nu_offset.T, pairs, occ_coef,
        vir_coef.reshape(2, 16, NVIR),
    )


def solution(mesh):
    placed = (
        P(("occ", "ao"), None),
        P(("occ", "ao"), None),
        P(("occ", "ao"), None),
        P(("occ", "ao"), None),
        P(),
        P("ao", None),
        P("ao", None),
    )
    return jax.shard_map(
        shards, mesh=mesh, in_specs=placed, out_specs=P("occ", "ao", None), check_vma=False
    )
```

```python
import jax
import jax.numpy as jnp
from jax import lax
from jax.experimental import pallas as pl
from jax.experimental.pallas import tpu as pltpu
from jax.sharding import PartitionSpec as P

NY, NX, NZ = 8, 4, 2
N_AO, N_OCC = 64, 8
TILES = 192
LANES = 256
CAP = 4
SLOTS = N_OCC * CAP
PAIRS = 32
P_LOC = PAIRS // N_OCC
NVIR = 1792
B_LOC = NVIR // N_AO
B_PAD = 32
CHUNK = 256
MESH = pl.DeviceIdType.MESH
F32, BF16, I32 = jnp.float32, jnp.bfloat16, jnp.int32


def remote(src, dst, send, recv, occ, ao):
    return pltpu.make_async_remote_copy(
        src_ref=src, dst_ref=dst, send_sem=send, recv_sem=recv,
        device_id=(occ, ao), device_id_type=MESH,
    )


def dot(a, b, dims=((1,), (0,))):
    return lax.dot_general(a, b, (dims, ((), ())), preferred_element_type=F32)


def iota(shape, dim):
    return lax.broadcasted_iota(I32, shape, dim)


def each(lo, hi, body, unroll=1):
    def step(k, carry):
        body(k)
        return carry

    lax.fori_loop(lo, hi, step, 0, unroll=unroll)


def kernel(
    ints_ref, owner_ref, blocks_ref, nuo_ref, pairs_ref, occ_ref, vir_ref,
    out_ref,
    cols, cols_f, vir, virp, flat, diag, expand, dens, part, s1, r1, meta, ids_o, sf, s2, r2, ids_s, ids_r,
    hot, hf, hb, vt, vs, vd, lhs, acc, places,
    g_s, g_r, y_s, y_r, z_s, z_r, x_s, x_r, c_s, c_r, m_s, m_r, a_s, a_r, b_s, b_r, i_s, i_r, v_s, v_r,
):
    occ = lax.axis_index("occ")
    ao = lax.axis_index("ao")
    half = lax.rem(occ, 2)
    sibling = occ + 1 - 2 * half
    zl = lax.rem(ao, NZ)
    x = lax.rem(ao // NZ, NX)
    y = ao // (NZ * NX)

    def ao_of(yy, xx, zz):
        return (yy * NX + xx) * NZ + zz

    xz = lax.rem(ao, 8)

    def wrap(t, n):
        return jnp.where(t >= n, t - n, t)

    Y_ORDER = (0, 1, 7, 2, 6, 3, 5, 4)

    def to_peers(body):
        for dy in Y_ORDER:
            base = wrap(y + dy, NY) * 8
            each(1 if dy == 0 else 0, 8, lambda q: body(dy * 8 + q, base + wrap(xz + q, 8)))

    OCC_ORDER = (1, 2, 3, 6, 7, 4, 5)

    def occ_to(k):
        return wrap(occ // 2 + k // 2, 4) * 2 + (half + k % 2) % 2

    def occ_from(k):
        return wrap(occ // 2 + 4 - k // 2, 4) * 2 + (half + k % 2) % 2

    def to_occ_peers(body):
        for k in OCC_ORDER:
            body(k, occ_to(k))

    barrier = pltpu.get_barrier_semaphore()

    to_occ_peers(
        lambda k, o: pl.semaphore_signal(barrier, inc=1, device_id=(o, ao), device_id_type=MESH)
    )
    to_peers(lambda k, a: pl.semaphore_signal(barrier, inc=1, device_id=(occ, a), device_id_type=MESH))
    ao_z = ao_of(y, x, 1 - zl)
    up, down = wrap(occ + 2 * zl, N_OCC), wrap(occ + 6 * (1 - zl), N_OCC)
    pl.semaphore_signal(
        barrier, inc=1, device_id=(wrap(occ + 6 - 4 * zl, N_OCC), ao_z), device_id_type=MESH
    )

    pick = (iota((256, 128), 0) == jnp.broadcast_to(pairs_ref[...], (256, 128))).astype(F32).astype(BF16)
    sel = dot(occ_ref[...], pick)
    cols[ao] = jnp.where(iota((16, 128), 1) < 64, sel[:16], sel[16:]).astype(BF16)

    def padded(row, fill):
        return jnp.concatenate([row.astype(F32), jnp.full((1, LANES - TILES), fill, F32)], axis=1)

    owner = padded(owner_ref[...], -1.0)
    mu = blocks_ref[0:1]
    la = blocks_ref[1:2]
    rows = jnp.concatenate(
        [
            owner,
            padded((mu // 4) * 2 + mu % 2, -1.0),
            padded((mu // 2) % 2, 0.0),
            padded((la // 4) * 2 + la % 2, -1.0),
            padded((la // 2) % 2, 0.0),
            jnp.zeros((3, LANES), F32),
        ],
        axis=0,
    )
    upright = jnp.concatenate([rows, jnp.zeros((120, LANES), F32)], axis=0).T
    same = (upright[:, 0:1] == owner) & (iota((LANES, LANES), 0) < iota((LANES, LANES), 1))
    rank = jnp.sum(jnp.where(same, 1.0, 0.0), axis=0, keepdims=True)
    key = jnp.where(owner < 0.0, 256.0, rank * N_AO + owner)
    meta[occ] = jnp.concatenate(
        [key, padded(blocks_ref[2:3], 0.0), padded(nuo_ref[...], 0.0), jnp.zeros((5, LANES), F32)], axis=0
    )

    def expansion(n):
        k = iota((256, 128), 1) % 64
        p = n * 2 + iota((256, 128), 1) // 64
        d = iota((256, 128), 0) // 32
        hit = (iota((256, 128), 0) % 32) == p
        left = hit & (d == (k % 32) // 4)
        right = hit & (d == (k % 4) * 2 + k // 32)
        expand[0, n] = jnp.where(left, 1.0, 0.0).astype(BF16)
        expand[1, n] = jnp.where(right, 1.0, 0.0).astype(BF16)

    each(0, 16, expansion)

    for kk in range(32):
        flat[kk * TILES:(kk + 1) * TILES] = ints_ref[:, kk * 128:(kk + 1) * 128].astype(F32)
    low = iota((32, 128), 1) < 64

    def place(t):
        block = flat[pl.ds(t, 32, stride=TILES), :]
        turned = pltpu.roll(block, 64, 1)
        zero = jnp.zeros_like(block)
        diag[t] = jnp.concatenate(
            [
                jnp.where(low, block, zero),
                jnp.where(low, turned, zero),
                jnp.where(low, zero, turned),
                jnp.where(low, zero, block),
            ],
            axis=0,
        ).astype(BF16)

    each(0, TILES, place, unroll=4)

    pl.semaphore_wait(barrier, N_AO + N_OCC - 1)

    def g_copy(k, a=0):
        return remote(cols.at[ao], cols.at[ao], g_s.at[k], g_r.at[k], occ, a)

    def m_copy(k, o=0):
        return remote(meta.at[occ], meta.at[occ], m_s.at[k], m_r.at[k], o, ao)

    def y_copy(k):
        return remote(
            vir_ref.at[half], vir.at[y, x, zl, half], y_s.at[k], y_r.at[k], occ, ao_of(wrap(y + k, NY), x, zl)
        )

    to_peers(lambda k, a: g_copy(k, a).start())
    to_occ_peers(lambda k, o: m_copy(k, o).start())
    vir[y, x, zl, half] = vir_ref[half]

    each(1, N_AO, lambda k: g_copy(k).wait())
    each(1, NY, lambda k: y_copy(k).start())
    cols_f[...] = cols[...].astype(F32).reshape(N_AO * 16, 128)
    table = jnp.concatenate(
        [cols_f[pl.ds(d, 128, stride=8), :].astype(BF16) for d in range(8)], axis=1
    )

    lane = iota((TILES, 1024), 1)

    def chosen(which):
        at = upright[:TILES, 1 + 2 * which:2 + 2 * which]
        part_of = upright[:TILES, 2 + 2 * which:3 + 2 * which]
        hot_rows = (iota((TILES, 128), 1).astype(F32) == at)
        got = dot(jnp.where(hot_rows, 1.0, 0.0).astype(BF16), table)
        keep = ((lane // 64) % 2).astype(F32) == part_of
        keep = keep & ((lane // 32) % 2 == which)
        got = jnp.where(keep, got, 0.0)
        folded = []
        for g in range(2):
            total = jnp.zeros((TILES, 128), F32)
            for d in range(4):
                piece = got[:, (g * 4 + d) * 128:(g * 4 + d + 1) * 128]
                piece = piece + pltpu.roll(piece, 64, 1)
                piece = piece + pltpu.roll(piece, 32, 1)
                total = jnp.where(iota((TILES, 128), 1) // 32 == d, piece, total)
            folded.append(total)
        return jnp.concatenate(folded, axis=1).astype(BF16)

    left = chosen(0)
    right = chosen(1)
    for n in range(16):
        dens[n * TILES:(n + 1) * TILES] = dot(left, expand[0, n]) * dot(right, expand[1, n])

    def multiply(t):
        d = dens[pl.ds(t, 16, stride=TILES), :]
        hi = d.astype(BF16)
        lo = (d - hi.astype(F32)).astype(BF16)
        got = dot(jnp.concatenate([hi, lo], axis=0), diag[t])
        part[pl.ds(t, 16, stride=TILES), :] = got[:16] + got[16:]

    each(0, TILES, multiply, unroll=8)
    def a_copy(n, k, o=0):
        return remote(s1.at[n, o], r1.at[n, occ], a_s.at[n, k], a_r.at[n, k], o, ao)

    for n in range(2):
        for o in range(N_OCC):
            at = (2 * o + n) * TILES
            s1[n, o] = part[at:at + TILES].astype(BF16)
        to_occ_peers(lambda k, o: a_copy(n, k, o).start())
        r1[n, occ] = s1[n, occ]

    each(1, NY, lambda k: y_copy(k).wait())
    to_r, to_l = wrap(x + 1, NX), wrap(x + NX - 1, NX)

    def x_copy(n, block, lo, hi, to):
        ref = vir.at[lo:hi, block, zl, half]
        return remote(ref, ref, x_s.at[n], x_r.at[n], occ, ao_of(y, to, zl))

    x_near, x_far = [], []
    for h in range(2):
        lo, hi = h * 4, h * 4 + 4
        x_near.append((x_copy(4 * h, x, lo, hi, to_r), x_copy(4 * h + 1, x, lo, hi, to_l)))
        x_far.append((x_copy(4 * h + 2, to_l, lo, lo + 2, to_r), x_copy(4 * h + 3, to_r, lo + 2, hi, to_l)))
    for h in range(2):
        for copy in x_near[h]:
            copy.start()
    to_occ_peers(lambda k, o: m_copy(k, o).wait())
    for h in range(2):
        for i in range(2):
            x_near[h][i].wait_recv()
            x_far[h][i].start()

    def z_copy(n):
        ref = vir.at[n * 4:n * 4 + 4, :, zl, half]
        return remote(ref, ref, z_s.at[n], z_r.at[n], (up, down)[n], ao_z)

    def c_copy(n, lo, hi, zz):
        ref = vir.at[lo:hi, :, zz, half]
        return remote(ref, ref, c_s.at[n], c_r.at[n], sibling, ao)

    z_copies = [z_copy(0), z_copy(1)]
    c_copies = [c_copy(0, 0, NY, zl), c_copy(1, 0, 4, 1 - zl), c_copy(2, 4, NY, 1 - zl)]

    def sort(n):
        for k in (0,) + OCC_ORDER:
            o = occ_from(k)
            if k > 0:
                a_copy(n, k).wait_recv()
            if n == 0:
                info = meta[o]
                hot_slots = jnp.where(
                    iota((256, LANES), 0).astype(F32) == info[0:1], 1.0, 0.0
                ).astype(BF16)
                places[o] = hot_slots
                names = dot(info.astype(BF16), hot_slots, ((1,), (1,)))
                ids_o[pl.ds(o, 1), :] = names[2:3] * 256.0 + names[1:2]
            else:
                hot_slots = places[o]
            got = dot(hot_slots[:, :TILES], r1[n, o])
            for r in range(CAP):
                sf[n, pl.ds(r * N_OCC + o, N_AO, stride=SLOTS), :] = got[r * 64:(r + 1) * 64]
        s2[n] = sf[n].astype(BF16).reshape(N_AO, SLOTS, 128)

    def b_copy(n, k, a=0):
        return remote(s2.at[n, a], r2.at[n, ao], b_s.at[n, k], b_r.at[n, k], occ, a)

    def i_copy(k, a=0):
        return remote(ids_s.at[a], ids_r.at[ao], i_s.at[k], i_r.at[k], occ, a)

    def start_first(k, a):
        i_copy(k, a).start()
        b_copy(0, k, a).start()

    def end_first(k):
        i_copy(k).wait()
        b_copy(0, k).wait()

    sort(0)
    turned_ids = jnp.concatenate([ids_o[...], jnp.zeros((120, 256), F32)], axis=0).T
    wide = jnp.zeros((N_AO, 128), F32)
    for r in range(CAP):
        wide = wide + pltpu.roll(turned_ids[r * 64:(r + 1) * 64], r * N_OCC, 1)
    ids_s[...] = wide.reshape(N_AO, 1, 128)
    to_peers(start_first)
    r2[0, ao] = s2[0, ao]
    ids_r[ao] = ids_s[ao]
    for h in range(2):
        for copy in x_far[h]:
            copy.wait_recv()
    for copy in z_copies:
        copy.start()
    c_copies[0].start()
    sort(1)
    to_peers(lambda k, a: b_copy(1, k, a).start())
    r2[1, ao] = s2[1, ao]

    def mark(s):
        names = jnp.broadcast_to(ids_r[s], (SLOTS, 128))
        name = jnp.sum(jnp.where(iota((SLOTS, 128), 0) == iota((SLOTS, 128), 1), names, 0.0), axis=1, keepdims=True)
        hot[s] = jnp.where(iota((SLOTS, 1024), 1).astype(F32) == name, 1.0, 0.0).astype(BF16)

    def collect(n):
        got_rows = r2[n].reshape(N_AO * SLOTS, 128)
        for m in range(4):
            total = dot(got_rows, hot[:, :, m * 256:(m + 1) * 256].reshape(N_AO * SLOTS, 256), ((0,), (0,)))
            hf[2 * m, n * 128:(n + 1) * 128] = total[:, :128]
            hf[2 * m + 1, n * 128:(n + 1) * 128] = total[:, 128:]

    each(1, N_AO, end_first)
    each(0, N_AO, mark, unroll=2)
    collect(0)
    for n in range(2):
        z_copies[n].wait_recv()
        c_copies[n + 1].start()
    each(1, N_AO, lambda k: b_copy(1, k).wait())
    collect(1)
    for copy in c_copies:
        copy.wait_recv()

    order = jnp.where(
        iota((256, 256), 1) == (iota((256, 256), 0) % 32) * 8 + iota((256, 256), 0) // 32, 1.0, 0.0
    ).astype(BF16)

    def chunk(n):
        return pl.ds(pl.multiple_of(n * CHUNK, CHUNK), CHUNK)

    def reorder(n):
        for j in range(NY):
            got = dot(order, vir[j, :, :, :, :, chunk(n)].reshape(256, CHUNK)).astype(BF16)
            for si in range(8):
                virp[si * 256 + j * 32:si * 256 + (j + 1) * 32, chunk(n)] = got[si * 32:(si + 1) * 32]

    each(0, NVIR // CHUNK, reorder)

    for si in range(8):
        for m in range(2):
            hb[:, si * 256 + m * 128:si * 256 + (m + 1) * 128] = jnp.concatenate(
                [hf[2 * n + m, pl.ds(p * 64 + si, 8, stride=8), :] for p in range(P_LOC) for n in range(4)], axis=0
            ).astype(BF16)

    def v_copy(k, a=0):
        return remote(vs.at[a], vd.at[ao], v_s.at[k], v_r.at[k], occ, a)

    def first(n):
        rows_v = dot(hb[...], virp[:, chunk(n)]).astype(BF16).astype(F32)
        vt[chunk(n)] = rows_v.T

    each(0, NVIR // CHUNK, first)
    vt[NVIR:] = jnp.zeros((8, 128), F32)
    for s in range(N_AO):
        vs[s] = vt[s * B_LOC:s * B_LOC + B_PAD].astype(BF16)
    to_peers(lambda k, a: v_copy(k, a).start())
    vd[ao] = vs[ao]

    quarter = iota((B_PAD, 128), 1) // 32

    def second(dy):
        sy = wrap(y + NY - dy, NY)
        each(1 if dy == 0 else 0, 8, lambda q: v_copy(dy * 8 + q).wait())
        for g in range(2):
            got = [vd[sy * 8 + 4 * g + s].astype(F32) for s in range(4)]
            for p in range(P_LOC):
                mixed = jnp.zeros((B_PAD, 128), F32)
                for s in range(4):
                    shift = ((s - p) % 4) * 32
                    piece = pltpu.roll(got[s], shift, 1) if shift else got[s]
                    mixed = jnp.where(quarter == s, piece, mixed)
                lhs[p * B_PAD:(p + 1) * B_PAD, g * 128:(g + 1) * 128] = mixed.astype(BF16)

        acc[...] += dot(lhs[...], vir[sy].reshape(256, NVIR))

    acc[...] = jnp.zeros_like(acc)
    for dy in Y_ORDER:
        second(dy)
    for p in range(P_LOC):
        out_ref[p] = acc[p * B_PAD:p * B_PAD + B_LOC]

    for n in range(2):
        each(1, N_OCC, lambda k: a_copy(n, k).wait_send())
    for copy in x_near[0] + x_near[1] + x_far[0] + x_far[1] + tuple(z_copies) + tuple(c_copies):
        copy.wait_send()


def shards(integrals, tile_owner, tile_blocks, nu_offset, pair_list, occ_coef, vir_coef):
    pairs = jnp.tile(pair_list.T.reshape(1, 2 * PAIRS), (1, 2))
    dma = pltpu.SemaphoreType.DMA
    vmem = pltpu.VMEM
    return pl.pallas_call(
        kernel,
        out_shape=jax.ShapeDtypeStruct((P_LOC, B_LOC, NVIR), F32),
        in_specs=[pl.BlockSpec(memory_space=pltpu.VMEM)] * 7,
        out_specs=pl.BlockSpec(memory_space=pltpu.VMEM),
        scratch_shapes=[
            vmem((N_AO, 16, 128), BF16),
            vmem((N_AO * 16, 128), F32),
            vmem((NY, NX, NZ, 2, 16, NVIR), BF16),
            vmem((N_AO * 32, NVIR), BF16),
            vmem((32 * TILES, 128), F32),
            vmem((TILES, 128, 128), BF16),
            vmem((2, 16, 256, 128), BF16),
            vmem((16 * TILES, 128), F32),
            vmem((16 * TILES, 128), F32),
            vmem((2, N_OCC, TILES, 128), BF16),
            vmem((2, N_OCC, TILES, 128), BF16),
            vmem((N_OCC, 8, LANES), F32),
            vmem((N_OCC, 256), F32),
            vmem((2, N_AO * SLOTS, 128), F32),
            vmem((2, N_AO, SLOTS, 128), BF16),
            vmem((2, N_AO, SLOTS, 128), BF16),
            vmem((N_AO, 1, 128), F32),
            vmem((N_AO, 1, 128), F32),
            vmem((N_AO, SLOTS, 1024), BF16),
            vmem((8, 256, 128), F32),
            vmem((128, 2048), BF16),
            vmem((NVIR + 8, 128), F32),
            vmem((N_AO, B_PAD, 128), BF16),
            vmem((N_AO, B_PAD, 128), BF16),
            vmem((128, 256), BF16),
            vmem((128, NVIR), F32),
            vmem((N_OCC, 256, LANES), BF16),
            dma((N_AO,)), dma((N_AO,)), dma((NY,)), dma((NY,)), dma((2,)), dma((2,)),
            dma((8,)), dma((8,)), dma((3,)), dma((3,)), dma((N_OCC,)), dma((N_OCC,)),
            dma((2, N_OCC)), dma((2, N_OCC)), dma((2, N_AO)), dma((2, N_AO)),
            dma((N_AO,)), dma((N_AO,)), dma((N_AO,)), dma((N_AO,)),
        ],
        compiler_params=pltpu.CompilerParams(
            collective_id=0, has_side_effects=True, vmem_limit_bytes=60 * 1024 * 1024
        ),
    )(
        integrals, tile_owner.T, tile_blocks.T, nu_offset.T, pairs, occ_coef,
        vir_coef.reshape(2, 16, NVIR),
    )


def solution(mesh):
    placed = (
        P(("occ", "ao"), None),
        P(("occ", "ao"), None),
        P(("occ", "ao"), None),
        P(("occ", "ao"), None),
        P(),
        P("ao", None),
        P("ao", None),
    )
    return jax.shard_map(
        shards, mesh=mesh, in_specs=placed, out_specs=P("occ", "ao", None), check_vma=False
    )
```

```python
import jax
import jax.numpy as jnp
from jax import lax
from jax.experimental import pallas as pl
from jax.experimental.pallas import tpu as pltpu
from jax.sharding import PartitionSpec as P

NY, NX, NZ = 8, 4, 2
N_AO, N_OCC = 64, 8
TILES = 192
LANES = 256
CAP = 4
SLOTS = N_OCC * CAP
PAIRS = 32
P_LOC = PAIRS // N_OCC
NVIR = 1792
B_LOC = NVIR // N_AO
B_PAD = 32
CHUNK = 256
MESH = pl.DeviceIdType.MESH
F32, BF16, I32 = jnp.float32, jnp.bfloat16, jnp.int32


def remote(src, dst, send, recv, occ, ao):
    return pltpu.make_async_remote_copy(
        src_ref=src, dst_ref=dst, send_sem=send, recv_sem=recv,
        device_id=(occ, ao), device_id_type=MESH,
    )


def dot(a, b, dims=((1,), (0,))):
    return lax.dot_general(a, b, (dims, ((), ())), preferred_element_type=F32)


def iota(shape, dim):
    return lax.broadcasted_iota(I32, shape, dim)


def each(lo, hi, body, unroll=1):
    def step(k, carry):
        body(k)
        return carry

    lax.fori_loop(lo, hi, step, 0, unroll=unroll)


def kernel(
    ints_ref, owner_ref, blocks_ref, nuo_ref, pairs_ref, occ_ref, vir_ref,
    out_ref,
    cols, cols_f, vir, virp, flat, diag, expand, dens, part, s1, r1, meta, ids_o, sf, s2, r2, ids_s, ids_r,
    hot, hf, hb, vt, vs, vd, lhs, acc, places,
    g_s, g_r, y_s, y_r, z_s, z_r, x_s, x_r, c_s, c_r, m_s, m_r, a_s, a_r, b_s, b_r, i_s, i_r, v_s, v_r,
):
    occ = lax.axis_index("occ")
    ao = lax.axis_index("ao")
    half = lax.rem(occ, 2)
    sibling = occ + 1 - 2 * half
    zl = lax.rem(ao, NZ)
    x = lax.rem(ao // NZ, NX)
    y = ao // (NZ * NX)

    def ao_of(yy, xx, zz):
        return (yy * NX + xx) * NZ + zz

    xz = lax.rem(ao, 8)

    def wrap(t, n):
        return jnp.where(t >= n, t - n, t)

    Y_ORDER = (0, 1, 7, 2, 6, 3, 5, 4)

    def to_peers(body):
        for dy in Y_ORDER:
            base = wrap(y + dy, NY) * 8
            each(1 if dy == 0 else 0, 8, lambda q: body(dy * 8 + q, base + wrap(xz + q, 8)))

    OCC_ORDER = (1, 2, 3, 6, 7, 4, 5)

    def occ_to(k):
        return wrap(occ // 2 + k // 2, 4) * 2 + (half + k % 2) % 2

    def occ_from(k):
        return wrap(occ // 2 + 4 - k // 2, 4) * 2 + (half + k % 2) % 2

    def to_occ_peers(body):
        for k in OCC_ORDER:
            body(k, occ_to(k))

    barrier = pltpu.get_barrier_semaphore()

    to_occ_peers(
        lambda k, o: pl.semaphore_signal(barrier, inc=1, device_id=(o, ao), device_id_type=MESH)
    )
    to_peers(lambda k, a: pl.semaphore_signal(barrier, inc=1, device_id=(occ, a), device_id_type=MESH))
    ao_z = ao_of(y, x, 1 - zl)
    outer = wrap(occ + 6 - 4 * zl, N_OCC)
    pl.semaphore_signal(
        barrier, inc=1, device_id=(outer, ao_z), device_id_type=MESH
    )

    pick = (iota((256, 128), 0) == jnp.broadcast_to(pairs_ref[...], (256, 128))).astype(F32).astype(BF16)
    sel = dot(occ_ref[...], pick)
    cols[ao] = jnp.where(iota((16, 128), 1) < 64, sel[:16], sel[16:]).astype(BF16)

    def padded(row, fill):
        return jnp.concatenate([row.astype(F32), jnp.full((1, LANES - TILES), fill, F32)], axis=1)

    owner = padded(owner_ref[...], -1.0)
    mu = blocks_ref[0:1]
    la = blocks_ref[1:2]
    rows = jnp.concatenate(
        [
            owner,
            padded((mu // 4) * 2 + mu % 2, -1.0),
            padded((mu // 2) % 2, 0.0),
            padded((la // 4) * 2 + la % 2, -1.0),
            padded((la // 2) % 2, 0.0),
            jnp.zeros((3, LANES), F32),
        ],
        axis=0,
    )
    upright = jnp.concatenate([rows, jnp.zeros((120, LANES), F32)], axis=0).T
    same = (upright[:, 0:1] == owner) & (iota((LANES, LANES), 0) < iota((LANES, LANES), 1))
    rank = jnp.sum(jnp.where(same, 1.0, 0.0), axis=0, keepdims=True)
    key = jnp.where(owner < 0.0, 256.0, rank * N_AO + owner)
    shell = blocks_ref[2:3]
    shell = ((shell // 4) % 2) * 128 + (shell // 8) * 4 + shell % 4
    meta[occ] = jnp.concatenate(
        [key, padded(shell, 0.0), padded(nuo_ref[...], 0.0), jnp.zeros((5, LANES), F32)], axis=0
    )

    def expansion(n):
        k = iota((256, 128), 1) % 64
        p = n * 2 + iota((256, 128), 1) // 64
        d = iota((256, 128), 0) // 32
        hit = (iota((256, 128), 0) % 32) == p
        left = hit & (d == (k % 32) // 4)
        right = hit & (d == (k % 4) * 2 + k // 32)
        expand[0, n] = jnp.where(left, 1.0, 0.0).astype(BF16)
        expand[1, n] = jnp.where(right, 1.0, 0.0).astype(BF16)

    each(0, 16, expansion)

    for kk in range(32):
        flat[kk * TILES:(kk + 1) * TILES] = ints_ref[:, kk * 128:(kk + 1) * 128].astype(F32)
    low = iota((32, 128), 1) < 64

    def place(t):
        block = flat[pl.ds(t, 32, stride=TILES), :]
        turned = pltpu.roll(block, 64, 1)
        zero = jnp.zeros_like(block)
        diag[t] = jnp.concatenate(
            [
                jnp.where(low, block, zero),
                jnp.where(low, turned, zero),
                jnp.where(low, zero, turned),
                jnp.where(low, zero, block),
            ],
            axis=0,
        ).astype(BF16)

    each(0, TILES, place, unroll=4)

    pl.semaphore_wait(barrier, N_AO + N_OCC - 1)

    def g_copy(k, a=0):
        return remote(cols.at[ao], cols.at[ao], g_s.at[k], g_r.at[k], occ, a)

    def m_copy(k, o=0):
        return remote(meta.at[occ], meta.at[occ], m_s.at[k], m_r.at[k], o, ao)

    def y_copy(k):
        return remote(
            vir_ref.at[half], vir.at[y, x, zl, half], y_s.at[k], y_r.at[k], occ, ao_of(wrap(y + k, NY), x, zl)
        )

    to_peers(lambda k, a: g_copy(k, a).start())
    to_occ_peers(lambda k, o: m_copy(k, o).start())
    vir[y, x, zl, half] = vir_ref[half]

    each(1, NY, lambda k: y_copy(k).start())
    each(1, N_AO, lambda k: g_copy(k).wait())
    cols_f[...] = cols[...].astype(F32).reshape(N_AO * 16, 128)
    table = jnp.concatenate(
        [cols_f[pl.ds(d, 128, stride=8), :].astype(BF16) for d in range(8)], axis=1
    )

    lane = iota((TILES, 1024), 1)

    def chosen(which):
        at = upright[:TILES, 1 + 2 * which:2 + 2 * which]
        part_of = upright[:TILES, 2 + 2 * which:3 + 2 * which]
        hot_rows = (iota((TILES, 128), 1).astype(F32) == at)
        got = dot(jnp.where(hot_rows, 1.0, 0.0).astype(BF16), table)
        keep = ((lane // 64) % 2).astype(F32) == part_of
        keep = keep & ((lane // 32) % 2 == which)
        got = jnp.where(keep, got, 0.0)
        folded = []
        for g in range(2):
            total = jnp.zeros((TILES, 128), F32)
            for d in range(4):
                piece = got[:, (g * 4 + d) * 128:(g * 4 + d + 1) * 128]
                piece = piece + pltpu.roll(piece, 64, 1)
                piece = piece + pltpu.roll(piece, 32, 1)
                total = jnp.where(iota((TILES, 128), 1) // 32 == d, piece, total)
            folded.append(total)
        return jnp.concatenate(folded, axis=1).astype(BF16)

    left = chosen(0)
    right = chosen(1)
    for n in range(16):
        dens[n * TILES:(n + 1) * TILES] = dot(left, expand[0, n]) * dot(right, expand[1, n])

    def multiply(t):
        d = dens[pl.ds(t, 16, stride=TILES), :]
        hi = d.astype(BF16)
        lo = (d - hi.astype(F32)).astype(BF16)
        got = dot(jnp.concatenate([hi, lo], axis=0), diag[t])
        part[pl.ds(t, 16, stride=TILES), :] = got[:16] + got[16:]

    each(0, TILES, multiply, unroll=8)
    def a_copy(n, k, o=0):
        return remote(s1.at[n, o], r1.at[n, occ], a_s.at[n, k], a_r.at[n, k], o, ao)

    for n in range(2):
        for o in range(N_OCC):
            at = (2 * o + n) * TILES
            s1[n, o] = part[at:at + TILES].astype(BF16)
        to_occ_peers(lambda k, o: a_copy(n, k, o).start())
        r1[n, occ] = s1[n, occ]

    each(1, NY, lambda k: y_copy(k).wait())
    to_r, to_l = wrap(x + 1, NX), wrap(x + NX - 1, NX)

    def x_copy(n, block, lo, hi, to):
        ref = vir.at[lo:hi, block, zl, half]
        return remote(ref, ref, x_s.at[n], x_r.at[n], occ, ao_of(y, to, zl))

    x_near, x_far = [], []
    for h in range(2):
        lo, hi = h * 4, h * 4 + 4
        x_near.append((x_copy(4 * h, x, lo, hi, to_r), x_copy(4 * h + 1, x, lo, hi, to_l)))
        x_far.append((x_copy(4 * h + 2, to_l, lo, lo + 2, to_r), x_copy(4 * h + 3, to_r, lo + 2, hi, to_l)))
    for h in range(2):
        for copy in x_near[h]:
            copy.start()
    to_occ_peers(lambda k, o: m_copy(k, o).wait())
    for h in range(2):
        for i in range(2):
            x_near[h][i].wait_recv()
            x_far[h][i].start()

    def z_copy(n):
        ref = vir.at[(0, 5)[n]:(5, NY)[n], :, zl, half]
        return remote(ref, ref, z_s.at[n], z_r.at[n], (outer, occ)[n], ao_z)

    def c_copy(n, lo, hi, zz):
        ref = vir.at[lo:hi, :, zz, half]
        return remote(ref, ref, c_s.at[n], c_r.at[n], sibling, ao)

    z_copies = [z_copy(0), z_copy(1)]
    c_copies = [c_copy(0, 0, NY, zl), c_copy(1, 0, 5, 1 - zl), c_copy(2, 5, NY, 1 - zl)]

    def sort(n):
        for k in (0,) + OCC_ORDER:
            o = occ_from(k)
            if k > 0:
                a_copy(n, k).wait_recv()
            if n == 0:
                info = meta[o]
                hot_slots = jnp.where(
                    iota((256, LANES), 0).astype(F32) == info[0:1], 1.0, 0.0
                ).astype(BF16)
                places[o] = hot_slots
                names = dot(info.astype(BF16), hot_slots, ((1,), (1,)))
                ids_o[pl.ds(o, 1), :] = names[2:3] * 256.0 + names[1:2]
            else:
                hot_slots = places[o]
            got = dot(hot_slots[:, :TILES], r1[n, o])
            for r in range(CAP):
                sf[n, pl.ds(r * N_OCC + o, N_AO, stride=SLOTS), :] = got[r * 64:(r + 1) * 64]
        s2[n] = sf[n].astype(BF16).reshape(N_AO, SLOTS, 128)

    def b_copy(n, k, a=0):
        return remote(s2.at[n, a], r2.at[n, ao], b_s.at[n, k], b_r.at[n, k], occ, a)

    def i_copy(k, a=0):
        return remote(ids_s.at[a], ids_r.at[ao], i_s.at[k], i_r.at[k], occ, a)

    def start_first(k, a):
        i_copy(k, a).start()
        b_copy(0, k, a).start()

    def end_first(k):
        i_copy(k).wait()
        b_copy(0, k).wait()

    sort(0)
    turned_ids = jnp.concatenate([ids_o[...], jnp.zeros((120, 256), F32)], axis=0).T
    wide = jnp.zeros((N_AO, 128), F32)
    for r in range(CAP):
        wide = wide + pltpu.roll(turned_ids[r * 64:(r + 1) * 64], r * N_OCC, 1)
    ids_s[...] = wide.reshape(N_AO, 1, 128)
    to_peers(start_first)
    r2[0, ao] = s2[0, ao]
    ids_r[ao] = ids_s[ao]
    for h in range(2):
        for copy in x_far[h]:
            copy.wait_recv()
    for copy in z_copies:
        copy.start()
    c_copies[0].start()
    sort(1)
    to_peers(lambda k, a: b_copy(1, k, a).start())
    r2[1, ao] = s2[1, ao]

    def mark(s):
        names = jnp.broadcast_to(ids_r[s], (SLOTS, 128))
        name = jnp.sum(jnp.where(iota((SLOTS, 128), 0) == iota((SLOTS, 128), 1), names, 0.0), axis=1, keepdims=True)
        hot[s] = jnp.where(iota((SLOTS, 1024), 1).astype(F32) == name, 1.0, 0.0).astype(BF16)

    def collect(n):
        got_rows = r2[n].reshape(N_AO * SLOTS, 128)
        for m in range(4):
            total = dot(got_rows, hot[:, :, m * 256:(m + 1) * 256].reshape(N_AO * SLOTS, 256), ((0,), (0,)))
            hf[2 * m, n * 128:(n + 1) * 128] = total[:, :128]
            hf[2 * m + 1, n * 128:(n + 1) * 128] = total[:, 128:]

    each(1, N_AO, end_first)
    each(0, N_AO, mark, unroll=2)
    collect(0)
    order = jnp.where(
        iota((128, 128), 1) == (iota((128, 128), 0) % 16) * 8 + iota((128, 128), 0) // 16, 1.0, 0.0
    ).astype(BF16)

    def chunk(n):
        return pl.ds(pl.multiple_of(n * CHUNK, CHUNK), CHUNK)

    def reorder(zz, lo, hi):
        def columns(n):
            for j in range(lo, hi):
                got = dot(order, vir[j, :, zz, :, :, chunk(n)].reshape(128, CHUNK)).astype(BF16)
                for si in range(8):
                    virp[zz, si * 128 + j * 16:si * 128 + (j + 1) * 16, chunk(n)] = got[si * 16:(si + 1) * 16]

        each(0, NVIR // CHUNK, columns)

    c_copies[0].wait_recv()
    reorder(zl, 0, NY)
    for n in range(2):
        z_copies[n].wait_recv()
        c_copies[n + 1].start()
    each(1, N_AO, lambda k: b_copy(1, k).wait())
    collect(1)
    for m in range(2):
        for si in range(8):
            hb[m, :, si * 128:(si + 1) * 128] = jnp.concatenate(
                [hf[2 * n + m, pl.ds(p * 64 + si, 8, stride=8), :] for p in range(P_LOC) for n in range(4)], axis=0
            ).astype(BF16)

    def v_copy(k, a=0):
        return remote(vs.at[a], vd.at[ao], v_s.at[k], v_r.at[k], occ, a)

    def first_own(n):
        acc[:, chunk(n)] = dot(hb[zl], virp[zl, :, chunk(n)])

    def first(n):
        rows_v = acc[:, chunk(n)] + dot(hb[1 - zl], virp[1 - zl, :, chunk(n)])
        vt[chunk(n)] = rows_v.astype(BF16).astype(F32).T

    each(0, NVIR // CHUNK, first_own)
    c_copies[1].wait_recv()
    reorder(1 - zl, 0, 5)
    c_copies[2].wait_recv()
    reorder(1 - zl, 5, NY)
    each(0, NVIR // CHUNK, first)
    vt[NVIR:] = jnp.zeros((8, 128), F32)
    for s in range(N_AO):
        vs[s] = vt[s * B_LOC:s * B_LOC + B_PAD].astype(BF16)
    to_peers(lambda k, a: v_copy(k, a).start())
    vd[ao] = vs[ao]

    quarter = iota((B_PAD, 128), 1) // 32

    def second(dy):
        sy = wrap(y + NY - dy, NY)
        each(1 if dy == 0 else 0, 8, lambda q: v_copy(dy * 8 + q).wait())
        for g in range(2):
            got = [vd[sy * 8 + 4 * g + s].astype(F32) for s in range(4)]
            for p in range(P_LOC):
                mixed = jnp.zeros((B_PAD, 128), F32)
                for s in range(4):
                    shift = ((s - p) % 4) * 32
                    piece = pltpu.roll(got[s], shift, 1) if shift else got[s]
                    mixed = jnp.where(quarter == s, piece, mixed)
                lhs[p * B_PAD:(p + 1) * B_PAD, g * 128:(g + 1) * 128] = mixed.astype(BF16)

        acc[...] += dot(lhs[...], vir[sy].reshape(256, NVIR))

    acc[...] = jnp.zeros_like(acc)
    for dy in Y_ORDER:
        second(dy)
    for p in range(P_LOC):
        out_ref[p] = acc[p * B_PAD:p * B_PAD + B_LOC]

    for n in range(2):
        each(1, N_OCC, lambda k: a_copy(n, k).wait_send())
    for copy in x_near[0] + x_near[1] + x_far[0] + x_far[1] + tuple(z_copies) + tuple(c_copies):
        copy.wait_send()


def shards(integrals, tile_owner, tile_blocks, nu_offset, pair_list, occ_coef, vir_coef):
    pairs = jnp.tile(pair_list.T.reshape(1, 2 * PAIRS), (1, 2))
    dma = pltpu.SemaphoreType.DMA
    vmem = pltpu.VMEM
    return pl.pallas_call(
        kernel,
        out_shape=jax.ShapeDtypeStruct((P_LOC, B_LOC, NVIR), F32),
        in_specs=[pl.BlockSpec(memory_space=pltpu.VMEM)] * 7,
        out_specs=pl.BlockSpec(memory_space=pltpu.VMEM),
        scratch_shapes=[
            vmem((N_AO, 16, 128), BF16),
            vmem((N_AO * 16, 128), F32),
            vmem((NY, NX, NZ, 2, 16, NVIR), BF16),
            vmem((2, N_AO * 16, NVIR), BF16),
            vmem((32 * TILES, 128), F32),
            vmem((TILES, 128, 128), BF16),
            vmem((2, 16, 256, 128), BF16),
            vmem((16 * TILES, 128), F32),
            vmem((16 * TILES, 128), F32),
            vmem((2, N_OCC, TILES, 128), BF16),
            vmem((2, N_OCC, TILES, 128), BF16),
            vmem((N_OCC, 8, LANES), F32),
            vmem((N_OCC, 256), F32),
            vmem((2, N_AO * SLOTS, 128), F32),
            vmem((2, N_AO, SLOTS, 128), BF16),
            vmem((2, N_AO, SLOTS, 128), BF16),
            vmem((N_AO, 1, 128), F32),
            vmem((N_AO, 1, 128), F32),
            vmem((N_AO, SLOTS, 1024), BF16),
            vmem((8, 256, 128), F32),
            vmem((2, 128, 1024), BF16),
            vmem((NVIR + 8, 128), F32),
            vmem((N_AO, B_PAD, 128), BF16),
            vmem((N_AO, B_PAD, 128), BF16),
            vmem((128, 256), BF16),
            vmem((128, NVIR), F32),
            vmem((N_OCC, 256, LANES), BF16),
            dma((N_AO,)), dma((N_AO,)), dma((NY,)), dma((NY,)), dma((2,)), dma((2,)),
            dma((8,)), dma((8,)), dma((3,)), dma((3,)), dma((N_OCC,)), dma((N_OCC,)),
            dma((2, N_OCC)), dma((2, N_OCC)), dma((2, N_AO)), dma((2, N_AO)),
            dma((N_AO,)), dma((N_AO,)), dma((N_AO,)), dma((N_AO,)),
        ],
        compiler_params=pltpu.CompilerParams(
            collective_id=0, has_side_effects=True, vmem_limit_bytes=60 * 1024 * 1024
        ),
    )(
        integrals, tile_owner.T, tile_blocks.T, nu_offset.T, pairs, occ_coef,
        vir_coef.reshape(2, 16, NVIR),
    )


def solution(mesh):
    placed = (
        P(("occ", "ao"), None),
        P(("occ", "ao"), None),
        P(("occ", "ao"), None),
        P(("occ", "ao"), None),
        P(),
        P("ao", None),
        P("ao", None),
    )
    return jax.shard_map(
        shards, mesh=mesh, in_specs=placed, out_specs=P("occ", "ao", None), check_vma=False
    )
```

```python
import jax
import jax.numpy as jnp
from jax import lax
from jax.experimental import pallas as pl
from jax.experimental.pallas import tpu as pltpu
from jax.sharding import PartitionSpec as P

NY, NX, NZ = 8, 4, 2
N_AO, N_OCC = 64, 8
TILES = 192
LANES = 256
CAP = 4
SLOTS = N_OCC * CAP
PAIRS = 32
P_LOC = PAIRS // N_OCC
NVIR = 1792
B_LOC = NVIR // N_AO
B_PAD = 32
CHUNK = 256
MESH = pl.DeviceIdType.MESH
F32, BF16, I32 = jnp.float32, jnp.bfloat16, jnp.int32


def remote(src, dst, send, recv, occ, ao):
    return pltpu.make_async_remote_copy(
        src_ref=src, dst_ref=dst, send_sem=send, recv_sem=recv,
        device_id=(occ, ao), device_id_type=MESH,
    )


def dot(a, b, dims=((1,), (0,))):
    return lax.dot_general(a, b, (dims, ((), ())), preferred_element_type=F32)


def iota(shape, dim):
    return lax.broadcasted_iota(I32, shape, dim)


def each(lo, hi, body, unroll=1):
    def step(k, carry):
        body(k)
        return carry

    lax.fori_loop(lo, hi, step, 0, unroll=unroll)


def kernel(
    ints_ref, owner_ref, blocks_ref, nuo_ref, pairs_ref, occ_ref, vir_ref,
    out_ref,
    cols, cols_f, vir, virp, flat, diag, expand, dens, part, s1, r1, meta, ids_o, sf, s2, r2, ids_s, ids_r,
    hot, hf, hb, vt, vs, vd, lhs, acc, places,
    g_s, g_r, y_s, y_r, z_s, z_r, x_s, x_r, c_s, c_r, m_s, m_r, a_s, a_r, b_s, b_r, i_s, i_r, v_s, v_r,
):
    occ = lax.axis_index("occ")
    ao = lax.axis_index("ao")
    half = lax.rem(occ, 2)
    sibling = occ + 1 - 2 * half
    zl = lax.rem(ao, NZ)
    x = lax.rem(ao // NZ, NX)
    y = ao // (NZ * NX)

    def ao_of(yy, xx, zz):
        return (yy * NX + xx) * NZ + zz

    xz = lax.rem(ao, 8)

    def wrap(t, n):
        return jnp.where(t >= n, t - n, t)

    Y_ORDER = (0, 1, 7, 2, 6, 3, 5, 4)

    def to_peers(body):
        for dy in Y_ORDER:
            base = wrap(y + dy, NY) * 8
            each(1 if dy == 0 else 0, 8, lambda q: body(dy * 8 + q, base + wrap(xz + q, 8)))

    OCC_ORDER = (1, 2, 3, 6, 7, 4, 5)

    def occ_to(k):
        return wrap(occ // 2 + k // 2, 4) * 2 + (half + k % 2) % 2

    def occ_from(k):
        return wrap(occ // 2 + 4 - k // 2, 4) * 2 + (half + k % 2) % 2

    def to_occ_peers(body):
        for k in OCC_ORDER:
            body(k, occ_to(k))

    barrier = pltpu.get_barrier_semaphore()

    to_occ_peers(
        lambda k, o: pl.semaphore_signal(barrier, inc=1, device_id=(o, ao), device_id_type=MESH)
    )
    to_peers(lambda k, a: pl.semaphore_signal(barrier, inc=1, device_id=(occ, a), device_id_type=MESH))
    ao_z = ao_of(y, x, 1 - zl)
    outer = wrap(occ + 6 - 4 * zl, N_OCC)
    pl.semaphore_signal(
        barrier, inc=1, device_id=(outer, ao_z), device_id_type=MESH
    )

    pick = (iota((256, 128), 0) == jnp.broadcast_to(pairs_ref[...], (256, 128))).astype(F32).astype(BF16)
    sel = dot(occ_ref[...], pick)
    cols[ao] = jnp.where(iota((16, 128), 1) < 64, sel[:16], sel[16:]).astype(BF16)

    def padded(row, fill):
        return jnp.concatenate([row.astype(F32), jnp.full((1, LANES - TILES), fill, F32)], axis=1)

    owner = padded(owner_ref[...], -1.0)
    mu = blocks_ref[0:1]
    la = blocks_ref[1:2]
    rows = jnp.concatenate(
        [
            owner,
            padded((mu // 4) * 2 + mu % 2, -1.0),
            padded((mu // 2) % 2, 0.0),
            padded((la // 4) * 2 + la % 2, -1.0),
            padded((la // 2) % 2, 0.0),
            jnp.zeros((3, LANES), F32),
        ],
        axis=0,
    )
    upright = jnp.concatenate([rows, jnp.zeros((120, LANES), F32)], axis=0).T
    same = (upright[:, 0:1] == owner) & (iota((LANES, LANES), 0) < iota((LANES, LANES), 1))
    rank = jnp.sum(jnp.where(same, 1.0, 0.0), axis=0, keepdims=True)
    key = jnp.where(owner < 0.0, 256.0, rank * N_AO + owner)
    shell = blocks_ref[2:3]
    shell = ((shell // 4) % 2) * 128 + (shell // 8) * 4 + shell % 4
    meta[occ] = jnp.concatenate(
        [key, padded(shell, 0.0), padded(nuo_ref[...], 0.0), jnp.zeros((5, LANES), F32)], axis=0
    )

    def expansion(n):
        k = iota((256, 128), 1) % 64
        p = n * 2 + iota((256, 128), 1) // 64
        d = iota((256, 128), 0) // 32
        hit = (iota((256, 128), 0) % 32) == p
        left = hit & (d == (k % 32) // 4)
        right = hit & (d == (k % 4) * 2 + k // 32)
        expand[0, n] = jnp.where(left, 1.0, 0.0).astype(BF16)
        expand[1, n] = jnp.where(right, 1.0, 0.0).astype(BF16)

    each(0, 16, expansion)

    for kk in range(32):
        flat[kk * TILES:(kk + 1) * TILES] = ints_ref[:, kk * 128:(kk + 1) * 128].astype(F32)
    low = iota((32, 128), 1) < 64

    def place(t):
        block = flat[pl.ds(t, 32, stride=TILES), :]
        turned = pltpu.roll(block, 64, 1)
        zero = jnp.zeros_like(block)
        diag[t] = jnp.concatenate(
            [
                jnp.where(low, block, zero),
                jnp.where(low, turned, zero),
                jnp.where(low, zero, turned),
                jnp.where(low, zero, block),
            ],
            axis=0,
        ).astype(BF16)

    each(0, TILES, place, unroll=4)

    pl.semaphore_wait(barrier, N_AO + N_OCC - 1)

    def g_copy(k, a=0):
        return remote(cols.at[ao], cols.at[ao], g_s.at[k], g_r.at[k], occ, a)

    def m_copy(k, o=0):
        return remote(meta.at[occ], meta.at[occ], m_s.at[k], m_r.at[k], o, ao)

    def y_copy(k):
        return remote(
            vir_ref.at[half], vir.at[y, x, zl, half], y_s.at[k], y_r.at[k], occ, ao_of(wrap(y + k, NY), x, zl)
        )

    to_peers(lambda k, a: g_copy(k, a).start())
    to_occ_peers(lambda k, o: m_copy(k, o).start())
    vir[y, x, zl, half] = vir_ref[half]

    each(1, NY, lambda k: y_copy(k).start())
    each(1, N_AO, lambda k: g_copy(k).wait())
    cols_f[...] = cols[...].astype(F32).reshape(N_AO * 16, 128)
    table = jnp.concatenate(
        [cols_f[pl.ds(d, 128, stride=8), :].astype(BF16) for d in range(8)], axis=1
    )

    lane = iota((TILES, 1024), 1)

    def chosen(which):
        at = upright[:TILES, 1 + 2 * which:2 + 2 * which]
        part_of = upright[:TILES, 2 + 2 * which:3 + 2 * which]
        hot_rows = (iota((TILES, 128), 1).astype(F32) == at)
        got = dot(jnp.where(hot_rows, 1.0, 0.0).astype(BF16), table)
        keep = ((lane // 64) % 2).astype(F32) == part_of
        keep = keep & ((lane // 32) % 2 == which)
        got = jnp.where(keep, got, 0.0)
        folded = []
        for g in range(2):
            total = jnp.zeros((TILES, 128), F32)
            for d in range(4):
                piece = got[:, (g * 4 + d) * 128:(g * 4 + d + 1) * 128]
                piece = piece + pltpu.roll(piece, 64, 1)
                piece = piece + pltpu.roll(piece, 32, 1)
                total = jnp.where(iota((TILES, 128), 1) // 32 == d, piece, total)
            folded.append(total)
        return jnp.concatenate(folded, axis=1).astype(BF16)

    left = chosen(0)
    right = chosen(1)
    for n in range(16):
        dens[n * TILES:(n + 1) * TILES] = dot(left, expand[0, n]) * dot(right, expand[1, n])

    def multiply(t):
        d = dens[pl.ds(t, 16, stride=TILES), :]
        hi = d.astype(BF16)
        lo = (d - hi.astype(F32)).astype(BF16)
        got = dot(jnp.concatenate([hi, lo], axis=0), diag[t])
        part[pl.ds(t, 16, stride=TILES), :] = got[:16] + got[16:]

    each(0, TILES, multiply, unroll=8)
    def a_copy(n, k, o=0):
        return remote(s1.at[n, o], r1.at[n, occ], a_s.at[n, k], a_r.at[n, k], o, ao)

    for n in range(2):
        for o in range(N_OCC):
            at = (2 * o + n) * TILES
            s1[n, o] = part[at:at + TILES].astype(BF16)
        to_occ_peers(lambda k, o: a_copy(n, k, o).start())
        r1[n, occ] = s1[n, occ]

    each(1, NY, lambda k: y_copy(k).wait())
    to_r, to_l = wrap(x + 1, NX), wrap(x + NX - 1, NX)

    def x_copy(n, block, lo, hi, to):
        ref = vir.at[lo:hi, block, zl, half]
        return remote(ref, ref, x_s.at[n], x_r.at[n], occ, ao_of(y, to, zl))

    x_near, x_far = [], []
    for h in range(2):
        lo, hi = h * 4, h * 4 + 4
        x_near.append((x_copy(4 * h, x, lo, hi, to_r), x_copy(4 * h + 1, x, lo, hi, to_l)))
        x_far.append((x_copy(4 * h + 2, to_l, lo, lo + 2, to_r), x_copy(4 * h + 3, to_r, lo + 2, hi, to_l)))
    for h in range(2):
        for copy in x_near[h]:
            copy.start()
    to_occ_peers(lambda k, o: m_copy(k, o).wait())
    for h in range(2):
        for i in range(2):
            x_near[h][i].wait_recv()
            x_far[h][i].start()

    def z_copy(n):
        ref = vir.at[(0, 5)[n]:(5, NY)[n], :, zl, half]
        return remote(ref, ref, z_s.at[n], z_r.at[n], (outer, occ)[n], ao_z)

    def c_copy(n, lo, hi, zz):
        ref = vir.at[lo:hi, :, zz, half]
        return remote(ref, ref, c_s.at[n], c_r.at[n], sibling, ao)

    z_copies = [z_copy(0), z_copy(1)]
    c_copies = [c_copy(0, 0, NY, zl), c_copy(1, 0, 5, 1 - zl), c_copy(2, 5, NY, 1 - zl)]

    def sort(n):
        for k in (0,) + OCC_ORDER:
            o = occ_from(k)
            if k > 0:
                a_copy(n, k).wait_recv()
            if n == 0:
                info = meta[o]
                hot_slots = jnp.where(
                    iota((256, LANES), 0).astype(F32) == info[0:1], 1.0, 0.0
                ).astype(BF16)
                places[o] = hot_slots
                names = dot(info.astype(BF16), hot_slots, ((1,), (1,)))
                ids_o[pl.ds(o, 1), :] = names[2:3] * 256.0 + names[1:2]
            else:
                hot_slots = places[o]
            got = dot(hot_slots[:, :TILES], r1[n, o])
            for r in range(CAP):
                sf[n, pl.ds(r * N_OCC + o, N_AO, stride=SLOTS), :] = got[r * 64:(r + 1) * 64]
        s2[n] = sf[n].astype(BF16).reshape(N_AO, SLOTS, 128)

    def b_copy(n, k, a=0):
        return remote(s2.at[n, a], r2.at[n, ao], b_s.at[n, k], b_r.at[n, k], occ, a)

    def i_copy(k, a=0):
        return remote(ids_s.at[a], ids_r.at[ao], i_s.at[k], i_r.at[k], occ, a)

    def start_first(k, a):
        i_copy(k, a).start()
        b_copy(0, k, a).start()

    def end_first(k):
        i_copy(k).wait()
        b_copy(0, k).wait()

    sort(0)
    turned_ids = jnp.concatenate([ids_o[...], jnp.zeros((120, 256), F32)], axis=0).T
    wide = jnp.zeros((N_AO, 128), F32)
    for r in range(CAP):
        wide = wide + pltpu.roll(turned_ids[r * 64:(r + 1) * 64], r * N_OCC, 1)
    ids_s[...] = wide.reshape(N_AO, 1, 128)
    to_peers(start_first)
    r2[0, ao] = s2[0, ao]
    ids_r[ao] = ids_s[ao]
    for h in range(2):
        for copy in x_far[h]:
            copy.wait_recv()
    for copy in z_copies:
        copy.start()
    c_copies[0].start()
    sort(1)
    to_peers(lambda k, a: b_copy(1, k, a).start())
    r2[1, ao] = s2[1, ao]

    def mark(s):
        names = jnp.broadcast_to(ids_r[s], (SLOTS, 128))
        name = jnp.sum(jnp.where(iota((SLOTS, 128), 0) == iota((SLOTS, 128), 1), names, 0.0), axis=1, keepdims=True)
        hot[s] = jnp.where(iota((SLOTS, 1024), 1).astype(F32) == name, 1.0, 0.0).astype(BF16)

    def collect(n):
        got_rows = r2[n].reshape(N_AO * SLOTS, 128)
        for m in range(4):
            total = dot(got_rows, hot[:, :, m * 256:(m + 1) * 256].reshape(N_AO * SLOTS, 256), ((0,), (0,)))
            hf[2 * m, n * 128:(n + 1) * 128] = total[:, :128]
            hf[2 * m + 1, n * 128:(n + 1) * 128] = total[:, 128:]

    each(1, N_AO, end_first)
    each(0, N_AO, mark, unroll=4)
    collect(0)
    order = jnp.where(
        iota((128, 128), 1) == (iota((128, 128), 0) % 16) * 8 + iota((128, 128), 0) // 16, 1.0, 0.0
    ).astype(BF16)

    def chunk(n):
        return pl.ds(pl.multiple_of(n * CHUNK, CHUNK), CHUNK)

    def reorder(zz, lo, hi):
        def columns(n):
            for j in range(lo, hi):
                got = dot(order, vir[j, :, zz, :, :, chunk(n)].reshape(128, CHUNK)).astype(BF16)
                for si in range(8):
                    virp[zz, si * 128 + j * 16:si * 128 + (j + 1) * 16, chunk(n)] = got[si * 16:(si + 1) * 16]

        each(0, NVIR // CHUNK, columns)

    c_copies[0].wait_recv()
    reorder(zl, 0, NY)
    for n in range(2):
        z_copies[n].wait_recv()
        c_copies[n + 1].start()
    c_copies[1].wait_recv()
    reorder(1 - zl, 0, 5)
    c_copies[2].wait_recv()
    reorder(1 - zl, 5, NY)
    each(1, N_AO, lambda k: b_copy(1, k).wait())
    collect(1)
    for m in range(2):
        for si in range(8):
            hb[m, :, si * 128:(si + 1) * 128] = jnp.concatenate(
                [hf[2 * n + m, pl.ds(p * 64 + si, 8, stride=8), :] for p in range(P_LOC) for n in range(4)], axis=0
            ).astype(BF16)

    def v_copy(k, a=0):
        return remote(vs.at[a], vd.at[ao], v_s.at[k], v_r.at[k], occ, a)

    def first_own(n):
        acc[:, chunk(n)] = dot(hb[zl], virp[zl, :, chunk(n)])

    def first(n):
        rows_v = acc[:, chunk(n)] + dot(hb[1 - zl], virp[1 - zl, :, chunk(n)])
        vt[chunk(n)] = rows_v.astype(BF16).astype(F32).T

    each(0, NVIR // CHUNK, first_own)
    each(0, NVIR // CHUNK, first)
    vt[NVIR:] = jnp.zeros((8, 128), F32)
    for s in range(N_AO):
        vs[s] = vt[s * B_LOC:s * B_LOC + B_PAD].astype(BF16)
    to_peers(lambda k, a: v_copy(k, a).start())
    vd[ao] = vs[ao]

    quarter = iota((B_PAD, 128), 1) // 32

    def second(dy):
        sy = wrap(y + NY - dy, NY)
        each(1 if dy == 0 else 0, 8, lambda q: v_copy(dy * 8 + q).wait())
        for g in range(2):
            got = [vd[sy * 8 + 4 * g + s].astype(F32) for s in range(4)]
            for p in range(P_LOC):
                mixed = jnp.zeros((B_PAD, 128), F32)
                for s in range(4):
                    shift = ((s - p) % 4) * 32
                    piece = pltpu.roll(got[s], shift, 1) if shift else got[s]
                    mixed = jnp.where(quarter == s, piece, mixed)
                lhs[p * B_PAD:(p + 1) * B_PAD, g * 128:(g + 1) * 128] = mixed.astype(BF16)

        acc[...] += dot(lhs[...], vir[sy].reshape(256, NVIR))

    acc[...] = jnp.zeros_like(acc)
    for dy in Y_ORDER:
        second(dy)
    for p in range(P_LOC):
        out_ref[p] = acc[p * B_PAD:p * B_PAD + B_LOC]

    for n in range(2):
        each(1, N_OCC, lambda k: a_copy(n, k).wait_send())
    for copy in x_near[0] + x_near[1] + x_far[0] + x_far[1] + tuple(z_copies) + tuple(c_copies):
        copy.wait_send()


def shards(integrals, tile_owner, tile_blocks, nu_offset, pair_list, occ_coef, vir_coef):
    pairs = jnp.tile(pair_list.T.reshape(1, 2 * PAIRS), (1, 2))
    dma = pltpu.SemaphoreType.DMA
    vmem = pltpu.VMEM
    return pl.pallas_call(
        kernel,
        out_shape=jax.ShapeDtypeStruct((P_LOC, B_LOC, NVIR), F32),
        in_specs=[pl.BlockSpec(memory_space=pltpu.VMEM)] * 7,
        out_specs=pl.BlockSpec(memory_space=pltpu.VMEM),
        scratch_shapes=[
            vmem((N_AO, 16, 128), BF16),
            vmem((N_AO * 16, 128), F32),
            vmem((NY, NX, NZ, 2, 16, NVIR), BF16),
            vmem((2, N_AO * 16, NVIR), BF16),
            vmem((32 * TILES, 128), F32),
            vmem((TILES, 128, 128), BF16),
            vmem((2, 16, 256, 128), BF16),
            vmem((16 * TILES, 128), F32),
            vmem((16 * TILES, 128), F32),
            vmem((2, N_OCC, TILES, 128), BF16),
            vmem((2, N_OCC, TILES, 128), BF16),
            vmem((N_OCC, 8, LANES), F32),
            vmem((N_OCC, 256), F32),
            vmem((2, N_AO * SLOTS, 128), F32),
            vmem((2, N_AO, SLOTS, 128), BF16),
            vmem((2, N_AO, SLOTS, 128), BF16),
            vmem((N_AO, 1, 128), F32),
            vmem((N_AO, 1, 128), F32),
            vmem((N_AO, SLOTS, 1024), BF16),
            vmem((8, 256, 128), F32),
            vmem((2, 128, 1024), BF16),
            vmem((NVIR + 8, 128), F32),
            vmem((N_AO, B_PAD, 128), BF16),
            vmem((N_AO, B_PAD, 128), BF16),
            vmem((128, 256), BF16),
            vmem((128, NVIR), F32),
            vmem((N_OCC, 256, LANES), BF16),
            dma((N_AO,)), dma((N_AO,)), dma((NY,)), dma((NY,)), dma((2,)), dma((2,)),
            dma((8,)), dma((8,)), dma((3,)), dma((3,)), dma((N_OCC,)), dma((N_OCC,)),
            dma((2, N_OCC)), dma((2, N_OCC)), dma((2, N_AO)), dma((2, N_AO)),
            dma((N_AO,)), dma((N_AO,)), dma((N_AO,)), dma((N_AO,)),
        ],
        compiler_params=pltpu.CompilerParams(
            collective_id=0, has_side_effects=True, vmem_limit_bytes=60 * 1024 * 1024
        ),
    )(
        integrals, tile_owner.T, tile_blocks.T, nu_offset.T, pairs, occ_coef,
        vir_coef.reshape(2, 16, NVIR),
    )


def solution(mesh):
    placed = (
        P(("occ", "ao"), None),
        P(("occ", "ao"), None),
        P(("occ", "ao"), None),
        P(("occ", "ao"), None),
        P(),
        P("ao", None),
        P("ao", None),
    )
    return jax.shard_map(
        shards, mesh=mesh, in_specs=placed, out_specs=P("occ", "ao", None), check_vma=False
    )
```
